256 devices in a mesh: dp: 8 (over z_hi, x), ctx: 32 (over y, z_lo, core).
Axes of the slice: x: 4, y: 4, z: 8 (z_hi: 2, z_lo: 4; z = z_hi * 4 + z_lo), core: 2. Of those that a mesh axis runs over, the one named last changes fastest.
Arguments:
- queries: bfloat16 [65536, 1792], P(('dp', 'ctx')), parts along dimension 0, may hold values from -8 to 8
- keys: bfloat16 [65536, 256], P(('dp', 'ctx')), parts along dimension 0, may hold values from -8 to 8
- values: bfloat16 [65536, 256], P(('dp', 'ctx')), parts along dimension 0, may hold values from -6 to 6
- output_gradient: bfloat16 [65536, 1792], P(('dp', 'ctx')), parts along dimension 0, may hold values from -6 to 6
- lengths: int32 [256], P('dp'), parts along dimension 0, may hold values from 1 to 768, 8192 in all
Outputs:
- attended: bfloat16 [65536, 1792], P(('dp', 'ctx')), parts along dimension 0
- grad_queries: bfloat16 [65536, 1792], P(('dp', 'ctx')), parts along dimension 0
- grad_keys: bfloat16 [65536, 256], P(('dp', 'ctx')), parts along dimension 0
- grad_values: bfloat16 [65536, 256], P(('dp', 'ctx')), parts along dimension 0
The draws below stay inside these ranges and needn't reach their ends.
There are 8 independent parts, one for each index of `dp`. The reference program is written for one: setup_inputs(seed, part) draws one part's arguments, and reference() takes and returns one part's arrays. A program takes and returns all parts, laid end to end along the dimension named above; each array names one. Nothing has to cross between parts.
Inputs may be any that keep to these rules, and one draw needn't show every extreme that they name: The lengths of a row sum to 8192; the longest is exactly 768.
All inputs are finite; a program needn't handle non-finite values.
Results may differ from the reference program's by a relative error of at most 0.029.
Values may be sent and summed in bfloat16 or wider, within the bound.
A program may use at most 192 MiB of HBM per device.

```python
import math
import jax
import jax.numpy as jnp
import numpy as np
from jax import lax

QUERY_HEADS = 14
KEY_VALUE_HEADS = 2
HEAD_SIZE = 128
DOCS = 32
TOKENS_PER_PART = 256
PACKED_LENGTH = 8192
LONGEST_DOC_LEN = 768


def draw_queries(key, part):
    key = jax.random.fold_in(key, 11)
    return jnp.clip(jax.random.normal(key, (PACKED_LENGTH, QUERY_HEADS * HEAD_SIZE), jnp.float32), -6.0, 6.0).astype(jnp.bfloat16)


def draw_keys(key, part):
    key = jax.random.fold_in(key, 13)
    return jnp.clip(jax.random.normal(key, (PACKED_LENGTH, KEY_VALUE_HEADS * HEAD_SIZE), jnp.float32), -6.0, 6.0).astype(jnp.bfloat16)


def steps_of(own_key, dims, pieces, smallest, high):
    level, own = 1.0, jax.random.fold_in(own_key, 6)
    for dim, blocks in pieces:
        draws = jnp.exp(jax.random.uniform(jax.random.fold_in(own, dim), (blocks,), jnp.float32, smallest / len(pieces), high / len(pieces)))
        level = level * jnp.repeat(draws, dims[dim] // blocks).reshape([-1 if axis == dim else 1 for axis in range(len(dims))])
    return level


def length_profile(amount, total, bound, skew):
    portions = [(1 << 20) // math.isqrt(standing ** skew) + 1 for standing in range(2, amount + 1)]
    spare, given = total - bound - (amount - 1), [1] * (amount - 1)
    while spare > 0:
        movable = [i for i in range(amount - 1) if given[i] < bound]
        whole, left = sum([portions[i] for i in movable]), spare
        for i in movable:
            more = min(bound - given[i], max(1, left * portions[i] // whole), spare)
            given[i] = given[i] + more
            spare = spare - more
    return np.array([bound] + given)


def ragged_sizes(rng, amount, total, most, skew):
    if amount == 2:
        one = jax.random.randint(rng, (), max(1, total - most), min(most, total - 1) + 1)
        return jnp.stack([one, total - one])
    tallies = jnp.asarray(length_profile(amount, total, most, skew), jnp.int32)
    pairs = (amount - 1) // 2
    donor, receiver = tallies[1:1 + 2 * pairs:2], tallies[2:2 + 2 * pairs:2]
    margin = jnp.minimum(donor - 1, most - receiver)
    passed = jax.random.randint(jax.random.fold_in(rng, 1), (pairs,), 0, 1 << 20) % (margin + 1)
    tallies = tallies.at[1:1 + 2 * pairs:2].set(donor - passed).at[2:2 + 2 * pairs:2].set(receiver + passed)
    return tallies[jax.random.permutation(jax.random.fold_in(rng, 2), amount)]


def gaussian(stream_key, shape, deviation, most, split=(), kind=jnp.bfloat16):
    gain = steps_of(stream_key, shape, split, -0.22, 0.18) if split else 1.0
    drawn = jax.random.normal(stream_key, shape, jnp.float32) * deviation * gain
    return jnp.minimum(jnp.maximum(drawn, -most), most).astype(kind)


def setup_inputs(seed: int = 0, part: int = 0) -> dict:
    streams_of = jax.random.split(jax.random.key(seed), 6)
    part_splits = jax.random.split(jax.random.fold_in(streams_of[5], part), 6)
    return {
        "queries": draw_queries(jax.random.fold_in(jax.random.fold_in(streams_of[5], part), 71), part),
        "keys": draw_keys(jax.random.fold_in(jax.random.fold_in(streams_of[5], part), 71), part),
        "values": gaussian(part_splits[2], (PACKED_LENGTH, KEY_VALUE_HEADS * HEAD_SIZE), 1.0, 6.0, ((0, 32),)),
        "output_gradient": gaussian(part_splits[3], (PACKED_LENGTH, QUERY_HEADS * HEAD_SIZE), 1.0, 6.0, ((0, 32),)),
        "lengths": ragged_sizes(part_splits[4], DOCS, PACKED_LENGTH, LONGEST_DOC_LEN, 2).astype(jnp.int32),
    }


NEGATIVE_FILL = -1e+30

def doc_ids(positions, lengths):
    ends = jnp.cumsum(lengths).astype(jnp.int32)
    return lax.optimization_barrier(jnp.sum((positions[:, None] >= ends[None, :]).astype(jnp.int32), axis=1))

def reference(queries, keys, values, output_gradient, lengths):
    window_width = LONGEST_DOC_LEN + TOKENS_PER_PART
    scale = 1.0 / math.sqrt(HEAD_SIZE)
    group_factor = QUERY_HEADS // KEY_VALUE_HEADS
    blocks = PACKED_LENGTH // TOKENS_PER_PART
    leading_part = jnp.zeros((LONGEST_DOC_LEN, KEY_VALUE_HEADS * HEAD_SIZE), keys.dtype)
    padded_keys = jnp.concatenate([leading_part, keys], 0)
    padded_values = jnp.concatenate([leading_part, values], 0)

    def step(carry, index):
        acc_keys, acc_vals = carry
        start_offset = (index * TOKENS_PER_PART).astype(jnp.int32)
        query_block = lax.dynamic_slice_in_dim(queries, start_offset, TOKENS_PER_PART, 0).astype(jnp.float32).reshape(TOKENS_PER_PART, KEY_VALUE_HEADS, group_factor, HEAD_SIZE)
        block_gradient = lax.dynamic_slice_in_dim(output_gradient, start_offset, TOKENS_PER_PART, 0).astype(jnp.float32).reshape(TOKENS_PER_PART, KEY_VALUE_HEADS, group_factor, HEAD_SIZE)
        key_window_rows = lax.dynamic_slice_in_dim(padded_keys, start_offset, window_width, 0).astype(jnp.float32).reshape(window_width, KEY_VALUE_HEADS, HEAD_SIZE)
        value_window_rows = lax.dynamic_slice_in_dim(padded_values, start_offset, window_width, 0).astype(jnp.float32).reshape(window_width, KEY_VALUE_HEADS, HEAD_SIZE)
        q_pos = start_offset + jnp.arange(TOKENS_PER_PART, dtype=jnp.int32)
        k_pos = start_offset - LONGEST_DOC_LEN + jnp.arange(window_width, dtype=jnp.int32)
        q_doc = doc_ids(q_pos, lengths)
        k_doc = doc_ids(k_pos, lengths)
        mask = (k_pos[None, :] <= q_pos[:, None]) & (k_pos[None, :] >= 0) & (q_doc[:, None] == k_doc[None, :])
        mask = mask[None, None]
        scores = jnp.einsum('rkgd,wkd->kgrw', query_block, key_window_rows) * scale
        masked = jnp.where(mask, scores, NEGATIVE_FILL)
        top = lax.optimization_barrier(jnp.max(masked, axis=-1, keepdims=True))
        lse = top + jnp.log(lax.optimization_barrier(jnp.sum(jnp.where(mask, jnp.exp(masked - top), 0.0), axis=-1, keepdims=True)))
        probs = jnp.where(mask, jnp.exp(scores - lse), 0.0)
        lower_bound = lax.optimization_barrier(probs.astype(jnp.bfloat16)).astype(jnp.float32)
        out = jnp.einsum('kgrw,wkd->rkgd', lower_bound, value_window_rows).astype(jnp.bfloat16)
        out_wide = lax.optimization_barrier(out).astype(jnp.float32)
        delta = jnp.transpose(lax.optimization_barrier(jnp.sum(block_gradient * out_wide, axis=-1)), (1, 2, 0))[..., None]
        dprob = jnp.einsum('rkgd,wkd->kgrw', block_gradient, value_window_rows)
        score_gradient = (probs * (dprob - delta) * scale).astype(jnp.bfloat16)
        score_gradient = lax.optimization_barrier(score_gradient).astype(jnp.float32)
        grad_q = jnp.einsum('kgrw,wkd->rkgd', score_gradient, key_window_rows).astype(jnp.bfloat16)
        key_gradient = jnp.einsum('cmsl,scme->lce', score_gradient, query_block).reshape(window_width, KEY_VALUE_HEADS * HEAD_SIZE)
        value_gradient = jnp.einsum('cmsl,scme->lce', lower_bound, block_gradient).reshape(window_width, KEY_VALUE_HEADS * HEAD_SIZE)
        acc_keys = lax.dynamic_update_slice_in_dim(acc_keys, lax.dynamic_slice_in_dim(acc_keys, start_offset, window_width, 0) + key_gradient, start_offset, 0)
        acc_vals = lax.dynamic_update_slice_in_dim(acc_vals, lax.dynamic_slice_in_dim(acc_vals, start_offset, window_width, 0) + value_gradient, start_offset, 0)
        return ((acc_keys, acc_vals), (out.reshape(TOKENS_PER_PART, QUERY_HEADS * HEAD_SIZE), grad_q.reshape(TOKENS_PER_PART, QUERY_HEADS * HEAD_SIZE)))
    initial_carry = (jnp.zeros((LONGEST_DOC_LEN + PACKED_LENGTH, KEY_VALUE_HEADS * HEAD_SIZE), jnp.float32), jnp.zeros((LONGEST_DOC_LEN + PACKED_LENGTH, KEY_VALUE_HEADS * HEAD_SIZE), jnp.float32))
    (acc_keys, acc_vals), (outs, grads) = lax.scan(step, initial_carry, jnp.arange(blocks, dtype=jnp.int32))
    attended = outs.reshape(PACKED_LENGTH, QUERY_HEADS * HEAD_SIZE)
    grad_queries = grads.reshape(PACKED_LENGTH, QUERY_HEADS * HEAD_SIZE)
    return (attended, grad_queries, acc_keys[LONGEST_DOC_LEN:].astype(jnp.bfloat16), acc_vals[LONGEST_DOC_LEN:].astype(jnp.bfloat16))
```

```python
import math

import jax
import jax.numpy as jnp
from jax import lax
from jax.experimental import pallas as pl
from jax.experimental.pallas import tpu as pltpu
from jax.sharding import PartitionSpec as P

QUERY_HEADS = 14
KEY_VALUE_HEADS = 2
HEAD = 128
GROUP = QUERY_HEADS // KEY_VALUE_HEADS
DOCS = 32
ROWS = 256
HALO = 3
WINDOW = (HALO + 1) * ROWS
NEGATIVE_FILL = -1e30
SCALE = 1.0 / math.sqrt(HEAD)
LOG2E_SCALE = math.log2(math.e) * SCALE
BF16 = jnp.bfloat16
F32 = jnp.float32
MESH = pl.DeviceIdType.MESH
VMEM = pl.BlockSpec(memory_space=pltpu.VMEM)
SMEM = pl.BlockSpec(memory_space=pltpu.SMEM)
ANY = pl.BlockSpec(memory_space=pl.ANY)


def dot_nn(a, b):
    return lax.dot_general(a, b, (((1,), (0,)), ((), ())), preferred_element_type=F32)


def dot_nt(a, b):
    return lax.dot_general(a, b, (((1,), (1,)), ((), ())), preferred_element_type=F32)


def ring(me, by, count):
    return lax.rem(me + by + count, count)


def greet(me, count, offsets):
    barrier = pltpu.get_barrier_semaphore()
    for by in offsets:
        pl.semaphore_signal(
            barrier, inc=1, device_id={"ctx": ring(me, by, count)}, device_id_type=MESH
        )
    pl.semaphore_wait(barrier, len(offsets))


def remote(src, dst, send, recv, target):
    return pltpu.make_async_remote_copy(
        src_ref=src,
        dst_ref=dst,
        send_sem=send,
        recv_sem=recv,
        device_id={"ctx": target},
        device_id_type=MESH,
    )


def gather_kernel(count, k_ref, v_ref, halo_ref, send_sem, recv_sem):
    me = lax.axis_index("ctx")
    core = lax.rem(me, 2)
    greet(me, count, (-2, -1, 1, 2))
    own = (k_ref, v_ref)
    ahead = [
        remote(own[c], halo_ref.at[1, c], send_sem.at[0, c], recv_sem.at[1, c], ring(me, 2, count))
        for c in range(2)
    ]
    for copy in ahead:
        copy.start()
    beside = [
        remote(own[c], halo_ref.at[0, c], send_sem.at[1, c], recv_sem.at[0, c], ring(me, 1, count))
        for c in range(2)
    ]
    to_next = [
        remote(
            halo_ref.at[1, c],
            halo_ref.at[2, c],
            send_sem.at[2, c],
            recv_sem.at[2, c],
            ring(me, 1, count),
        )
        for c in range(2)
    ]
    to_partner = [
        remote(
            halo_ref.at[1, c],
            halo_ref.at[0, c],
            send_sem.at[1, c],
            recv_sem.at[0, c],
            ring(me, -1, count),
        )
        for c in range(2)
    ]

    @pl.when(core == 0)
    def _():
        for copy in beside:
            copy.start()

    for c in range(2):
        ahead[c].wait_recv()
        to_next[c].start()

        @pl.when(core == 1)
        def _():
            to_partner[c].start()

    for c in range(2):
        beside[c].wait_recv()
        to_next[c].wait_recv()
        ahead[c].wait_send()
        beside[c].wait_send()
        to_next[c].wait_send()


def attention_kernel(
    len_ref, q_ref, k_ref, v_ref, halo_ref, do_ref,
    o_ref, dq_ref, part_ref, own_ref,
    bias, kw, vw, kt, vt, e_all, ds_all, q_all, do_all, s_buf,
):
    me = lax.axis_index("ctx")
    base = me * ROWS
    q_pos = base + lax.broadcasted_iota(jnp.int32, (1, ROWS), 1)
    start = jnp.zeros((1, ROWS), jnp.int32)
    total = jnp.int32(0)
    for d in range(DOCS):
        total = total + len_ref[d]
        start = jnp.where(q_pos >= total, total, start)
    k_pos = base - HALO * ROWS + lax.broadcasted_iota(jnp.int32, (WINDOW, ROWS), 0)
    bias[...] = jnp.where((k_pos <= q_pos) & (k_pos >= start), 0.0, NEGATIVE_FILL)
    for g in range(KEY_VALUE_HEADS):
        cols = slice(g * HEAD, (g + 1) * HEAD)
        for d in range(HALO):
            rows = slice((HALO - 1 - d) * ROWS, (HALO - d) * ROWS)
            kw[g, rows] = halo_ref[d, 0, :, cols]
            vw[g, rows] = halo_ref[d, 1, :, cols]
        kw[g, HALO * ROWS :] = k_ref[:, cols]
        vw[g, HALO * ROWS :] = v_ref[:, cols]
        kt[g] = kw[g].T
        vt[g] = vw[g].T

    def scores(h, live):
        g, slot = h // GROUP, h % GROUP
        cols = slice(h * HEAD, (h + 1) * HEAD)
        q_t = q_ref[:, cols].T
        q_all[h] = q_t
        s = dot_nn(kw[g], q_t) + bias[...]
        s_buf[h % 2] = s
        live["m"] = jnp.max(s, axis=0, keepdims=True)

    def soft(h, live):
        e = jnp.exp2((s_buf[h % 2] - live["m"]) * LOG2E_SCALE)
        live["r"] = 1.0 / jnp.sum(e, axis=0, keepdims=True)
        e_all[h] = e.astype(BF16)

    def out(h, live):
        g = h // GROUP
        cols = slice(h * HEAD, (h + 1) * HEAD)
        o_t = (dot_nn(vt[g], e_all[h]) * live["r"]).astype(BF16)
        o_ref[:, cols] = o_t.T
        do_t = do_ref[:, cols].T.astype(F32)
        live["delta"] = jnp.sum(do_t * o_t.astype(F32), axis=0, keepdims=True) * live["r"]
        do_all[h] = (do_t * live["r"]).astype(BF16)

    def back(h, live):
        g = h // GROUP
        dp = dot_nn(vw[g], do_all[h])
        ds_all[h] = (e_all[h].astype(F32) * (dp - live["delta"])).astype(BF16)

    def grad_q(h, live):
        g = h // GROUP
        cols = slice(h * HEAD, (h + 1) * HEAD)
        dq_ref[:, cols] = (dot_nn(kt[g], ds_all[h]) * SCALE).astype(BF16).T

    stages = (scores, soft, out, back, grad_q)
    lives = [dict() for _ in range(QUERY_HEADS)]
    for step in range(QUERY_HEADS + len(stages) - 1):
        for lag, stage in enumerate(stages):
            if 0 <= step - lag < QUERY_HEADS:
                stage(step - lag, lives[step - lag])

    for g in range(KEY_VALUE_HEADS):
        cols = slice(g * HEAD, (g + 1) * HEAD)
        for b in range(HALO + 1):
            rows = slice(b * ROWS, (b + 1) * ROWS)
            grad_k = jnp.zeros((ROWS, HEAD), F32)
            grad_v = jnp.zeros((ROWS, HEAD), F32)
            for h in range(g * GROUP, (g + 1) * GROUP):
                grad_k += dot_nt(ds_all[h, rows], q_all[h])
                grad_v += dot_nt(e_all[h, rows], do_all[h])
            if b == HALO:
                own_ref[0, :, cols] = grad_k * SCALE
                own_ref[1, :, cols] = grad_v
            else:
                part_ref[HALO - 1 - b, 0, :, cols] = (grad_k * SCALE).astype(BF16)
                part_ref[HALO - 1 - b, 1, :, cols] = grad_v.astype(BF16)


def scatter_kernel(
    count, part_ref, own_ref, gk_ref, gv_ref,
    total, from_partner, from_next, direct, back, send_sem, recv_sem,
):
    me = lax.axis_index("ctx")
    core = lax.rem(me, 2)
    greet(me, count, (-3, -2, -1, 1, 2, 3))
    chunks = [(c, pl.ds(r * 128, 128)) for c in range(2) for r in range(2)]
    grads = (gk_ref, gv_ref)

    @pl.when(core == 0)
    def _():
        relay, partner, last = [], [], []
        for n, (c, rows) in enumerate(chunks):
            relay.append(
                remote(
                    part_ref.at[2, c, rows], from_next.at[c, rows],
                    send_sem.at[0, n], recv_sem.at[0, n], ring(me, -2, count),
                )
            )
            partner.append(
                remote(
                    part_ref.at[1, c, rows], from_partner.at[c, rows],
                    send_sem.at[1, n], recv_sem.at[1, n], ring(me, 1, count),
                )
            )
            last.append(
                remote(
                    total.at[c, rows], back.at[c, rows],
                    send_sem.at[2, n], recv_sem.at[2, n], ring(me, -1, count),
                )
            )
            partner[n].start()
            relay[n].start()
        for n, (c, rows) in enumerate(chunks):
            partner[n].wait_recv()
            relay[n].wait_recv()
            total[c, rows] = (
                part_ref[0, c, rows].astype(F32)
                + from_partner[c, rows].astype(F32)
                + from_next[c, rows].astype(F32)
            ).astype(BF16)
            last[n].start()
        for n, (c, rows) in enumerate(chunks):
            remote(
                total.at[c, rows], direct.at[c, rows],
                send_sem.at[3, n], recv_sem.at[3, n], ring(me, 1, count),
            ).wait_recv()
            last[n].wait_recv()
            grads[c][rows, :] = (
                own_ref[c, rows] + direct[c, rows].astype(F32) + back[c, rows].astype(F32)
            ).astype(BF16)
        for n in range(len(chunks)):
            relay[n].wait_send()
            partner[n].wait_send()
            last[n].wait_send()

    @pl.when(core == 1)
    def _():
        first, partner, last = [], [], []
        for n, (c, rows) in enumerate(chunks):
            first.append(
                remote(
                    part_ref.at[0, c, rows], direct.at[c, rows],
                    send_sem.at[3, n], recv_sem.at[3, n], ring(me, -1, count),
                )
            )
            partner.append(
                remote(
                    part_ref.at[1, c, rows], from_partner.at[c, rows],
                    send_sem.at[1, n], recv_sem.at[1, n], ring(me, -1, count),
                )
            )
            last.append(
                remote(
                    total.at[c, rows], back.at[c, rows],
                    send_sem.at[2, n], recv_sem.at[2, n], ring(me, -3, count),
                )
            )
            partner[n].start()
        for n, (c, rows) in enumerate(chunks):
            partner[n].wait_recv()
            total[c, rows] = (
                part_ref[2, c, rows].astype(F32) + from_partner[c, rows].astype(F32)
            ).astype(BF16)
            last[n].start()
        for n in range(len(chunks)):
            first[n].start()
        for n, (c, rows) in enumerate(chunks):
            last[n].wait_recv()
            grads[c][rows, :] = (own_ref[c, rows] + back[c, rows].astype(F32)).astype(BF16)
        for n in range(len(chunks)):
            first[n].wait_send()
            partner[n].wait_send()
            last[n].wait_send()


def per_device(queries, keys, values, output_gradient, lengths):
    count = lax.axis_size("ctx")
    width = KEY_VALUE_HEADS * HEAD
    wide = QUERY_HEADS * HEAD
    halo = pl.pallas_call(
        lambda *refs: gather_kernel(count, *refs),
        out_shape=jax.ShapeDtypeStruct((HALO, 2, ROWS, width), BF16),
        in_specs=[ANY, ANY],
        out_specs=ANY,
        scratch_shapes=[pltpu.SemaphoreType.DMA((3, 2)), pltpu.SemaphoreType.DMA((3, 2))],
        compiler_params=pltpu.CompilerParams(collective_id=0, has_side_effects=True),
        name="gather_halo",
    )(keys, values)
    attended, grad_queries, part, own = pl.pallas_call(
        attention_kernel,
        out_shape=[
            jax.ShapeDtypeStruct((ROWS, wide), BF16),
            jax.ShapeDtypeStruct((ROWS, wide), BF16),
            jax.ShapeDtypeStruct((HALO, 2, ROWS, width), BF16),
            jax.ShapeDtypeStruct((2, ROWS, width), F32),
        ],
        in_specs=[SMEM] + [VMEM] * 5,
        out_specs=[VMEM] * 4,
        scratch_shapes=[
            pltpu.VMEM((WINDOW, ROWS), F32),
            pltpu.VMEM((KEY_VALUE_HEADS, WINDOW, HEAD), BF16),
            pltpu.VMEM((KEY_VALUE_HEADS, WINDOW, HEAD), BF16),
            pltpu.VMEM((KEY_VALUE_HEADS, HEAD, WINDOW), BF16),
            pltpu.VMEM((KEY_VALUE_HEADS, HEAD, WINDOW), BF16),
            pltpu.VMEM((QUERY_HEADS, WINDOW, ROWS), BF16),
            pltpu.VMEM((QUERY_HEADS, WINDOW, ROWS), BF16),
            pltpu.VMEM((QUERY_HEADS, HEAD, ROWS), BF16),
            pltpu.VMEM((QUERY_HEADS, HEAD, ROWS), BF16),
            pltpu.VMEM((2, WINDOW, ROWS), F32),
        ],
        compiler_params=pltpu.CompilerParams(vmem_limit_bytes=56 << 20),
        name="attention",
    )(lengths, queries, keys, values, halo, output_gradient)
    grad_keys, grad_values = pl.pallas_call(
        lambda *refs: scatter_kernel(count, *refs),
        out_shape=[jax.ShapeDtypeStruct((ROWS, width), BF16)] * 2,
        in_specs=[VMEM, VMEM],
        out_specs=[VMEM, VMEM],
        scratch_shapes=[pltpu.VMEM((2, ROWS, width), BF16)] * 5
        + [pltpu.SemaphoreType.DMA((4, 4)), pltpu.SemaphoreType.DMA((4, 4))],
        compiler_params=pltpu.CompilerParams(
            collective_id=1, has_side_effects=True, vmem_limit_bytes=32 << 20
        ),
        name="scatter_gradients",
    )(part, own)
    return attended, grad_queries, grad_keys, grad_values


def solution(mesh):
    split = P(("dp", "ctx"), None)
    return jax.shard_map(
        per_device,
        mesh=mesh,
        in_specs=(split, split, split, split, P("dp")),
        out_specs=(split, split, split, split),
        check_vma=False,
    )
```

```python
import functools
import math

import jax
import jax.numpy as jnp
from jax import lax
from jax.experimental import pallas as pl
from jax.experimental.pallas import tpu as pltpu
from jax.sharding import PartitionSpec as P

QUERY_HEADS = 14
KEY_VALUE_HEADS = 2
HEAD = 128
GROUP = QUERY_HEADS // KEY_VALUE_HEADS
SPAN = GROUP * HEAD
DOCS = 32
ROWS = 256
SLOTS = 5
PIECES = 4
PIECE_ROWS = ROWS // 2
NEGATIVE_FILL = -1e30
SCALE = 1.0 / math.sqrt(HEAD)
LOG2E_SCALE = math.log2(math.e) * SCALE
BF16 = jnp.bfloat16
F32 = jnp.float32
MESH = pl.DeviceIdType.MESH
SMEM = pl.BlockSpec(memory_space=pltpu.SMEM)
HBM = pl.BlockSpec(memory_space=pltpu.HBM)


def dot_nn(a, b):
    return lax.dot_general(a, b, (((1,), (0,)), ((), ())), preferred_element_type=F32)


def remote(src, dst, send, recv, target):
    return pltpu.make_async_remote_copy(
        src_ref=src, dst_ref=dst, send_sem=send, recv_sem=recv,
        device_id={"ctx": target}, device_id_type=MESH,
    )


def fused_kernel(
    count, len_ref, q_ref, k_ref, v_ref, do_ref,
    o_ref, dq_ref, gk_ref, gv_ref,
    kv, kv_t, q_nat, do_nat, q_t, do_t, e_all, m_pair, m_run, l_run, o_t, dq_t, delta, inv, starts,
    g_sum, s_buf, p_buf, ds_buf, bias, o_stage, dq_stage, g_out, g_relay, g_far, g_near, gk_buf, gv_buf,
    local_sem, kv_send, kv_recv, act_send, act_recv, out_send, out_recv, g_send, g_recv,
):
    me = lax.axis_index("ctx")
    core = lax.rem(me, 2)
    other = 1 - core
    chip = me // 2
    partner = me + 1 - 2 * core

    def device(step, which):
        return lax.rem(2 * chip + 2 * step + count, count) + which

    def head_cols(which):
        return pl.ds(pl.multiple_of(which * HEAD, HEAD), HEAD)

    def span_cols(which):
        return pl.ds(pl.multiple_of(which * SPAN, HEAD), SPAN)

    def piece(n):
        return n // 2, pl.ds((n % 2) * PIECE_ROWS, PIECE_ROWS)

    local = [
        pltpu.make_async_copy(q_ref.at[:, span_cols(core)], q_nat.at[core], local_sem.at[0]),
        pltpu.make_async_copy(do_ref.at[:, span_cols(core)], do_nat.at[core], local_sem.at[1]),
        pltpu.make_async_copy(k_ref.at[:, head_cols(core)], kv.at[core, 0], local_sem.at[2]),
        pltpu.make_async_copy(v_ref.at[:, head_cols(core)], kv.at[core, 1], local_sem.at[3]),
    ]
    for copy in local:
        copy.start()
    barrier = pltpu.get_barrier_semaphore()
    for target in (partner, device(-1, 0), device(-1, 1), device(1, 0), device(1, 1)):
        pl.semaphore_signal(barrier, inc=1, device_id={"ctx": target}, device_id_type=MESH)

    m_run[...] = jnp.full_like(m_run, NEGATIVE_FILL)
    l_run[...] = jnp.zeros_like(l_run)
    o_t[...] = jnp.zeros_like(o_t)
    dq_t[...] = jnp.zeros_like(dq_t)
    g_sum[...] = jnp.zeros_like(g_sum)
    for qs in range(2):
        q_pos = (2 * chip + qs) * ROWS + lax.broadcasted_iota(jnp.int32, (8, ROWS), 1)
        start = jnp.zeros((8, ROWS), jnp.int32)
        total = jnp.int32(0)
        for d in range(DOCS):
            total = total + len_ref[d]
            start = jnp.where(q_pos >= total, total, start)
        starts[qs] = start

    def turn_queries(qs):
        for h in range(GROUP):
            cols = slice(h * HEAD, (h + 1) * HEAD)
            q_t[qs, h] = q_nat[qs, :, cols].T
            do_t[qs, h] = do_nat[qs, :, cols].T

    def turn_keys(slot):
        kv_t[slot, 0] = kv[slot, 0].T
        kv_t[slot, 1] = kv[slot, 1].T

    def block_of(slot):
        return 2 * chip + jnp.where(slot < 2, slot, jnp.where(slot == 4, -3, slot - 4))

    def staged(stages, lives):
        for step in range(GROUP + len(stages) - 1):
            for lag, stage in enumerate(stages):
                if 0 <= step - lag < GROUP:
                    stage(step - lag, lives[step - lag])

    def forward(qs, slot, pair):
        q_pos = (2 * chip + qs) * ROWS + lax.broadcasted_iota(jnp.int32, (1, ROWS), 1)
        k_pos = block_of(slot) * ROWS + lax.broadcasted_iota(jnp.int32, (ROWS, ROWS), 0)
        inside = (k_pos <= q_pos) & (k_pos >= starts[qs, 0:1])
        bias[...] = jnp.where(inside, 0.0, NEGATIVE_FILL)

        def scores(h, live):
            s = dot_nn(kv[slot, 0], q_t[qs, h]) + bias[...]
            s_buf[h % 3] = s
            old = m_run[qs, h : h + 1]
            top = jnp.maximum(old, jnp.max(s, axis=0, keepdims=True))
            m_run[qs, h : h + 1] = top
            m_pair[pair, h : h + 1] = top
            live["top"] = top
            live["shrink"] = jnp.exp2((old - top) * LOG2E_SCALE)

        def soft(h, live):
            e = jnp.exp2((s_buf[h % 3] - live["top"]) * LOG2E_SCALE)
            l_run[qs, h : h + 1] = l_run[qs, h : h + 1] * live["shrink"] + jnp.sum(
                e, axis=0, keepdims=True
            )
            e_all[pair, :, h * ROWS : (h + 1) * ROWS] = e.astype(BF16)

        def out(h, live):
            e = e_all[pair, :, h * ROWS : (h + 1) * ROWS]
            o_t[qs, h] = o_t[qs, h] * live["shrink"] + dot_nn(kv_t[slot, 1], e)

        staged((scores, soft, out), [dict() for _ in range(GROUP)])

    def finish_forward(qs):
        for h in range(GROUP):
            r = 1.0 / l_run[qs, h : h + 1]
            low = (o_t[qs, h] * r).astype(BF16)
            o_stage[qs, :, h * HEAD : (h + 1) * HEAD] = low.T
            inv[qs, h : h + 1] = r
            delta[qs, h : h + 1] = jnp.sum(
                do_t[qs, h].astype(F32) * low.astype(F32), axis=0, keepdims=True
            )

    def backward(qs, slot, pair):
        def dprob(h, live):
            s_buf[h % 3] = dot_nn(kv[slot, 1], do_t[qs, h])

        def dscore(h, live):
            rows = slice(h * ROWS, (h + 1) * ROWS)
            one = slice(h, h + 1)
            factor = jnp.exp2((m_pair[pair, one] - m_run[qs, one]) * LOG2E_SCALE) * inv[qs, one]
            p = e_all[pair, :, rows].astype(F32) * factor
            p_buf[:, rows] = p.astype(BF16)
            ds_buf[:, rows] = (p * (s_buf[h % 3] - delta[qs, one])).astype(BF16)

        def grad(h, live):
            rows = slice(h * ROWS, (h + 1) * ROWS)
            cols = slice(h * HEAD, (h + 1) * HEAD)
            dq_t[qs, h] += dot_nn(kv_t[slot, 0], ds_buf[:, rows])
            g_sum[slot, 1] += dot_nn(p_buf[:, rows], do_nat[qs, :, cols])
            g_sum[slot, 0] += dot_nn(ds_buf[:, rows], q_nat[qs, :, cols])

        staged((dprob, dscore, grad), [dict() for _ in range(GROUP)])

    def finish_backward(qs):
        for h in range(GROUP):
            dq_stage[qs, :, h * HEAD : (h + 1) * HEAD] = (dq_t[qs, h] * SCALE).astype(BF16).T

    def grad_piece(slot, n):
        c, rows = piece(n)
        return g_sum[slot, c, rows] * (SCALE if c == 0 else 1.0)

    for copy in local:
        copy.wait()
    turn_queries(core)
    turn_keys(core)
    forward(core, core, 4 * core)
    pl.semaphore_wait(barrier, 5)

    own = (k_ref, v_ref)
    sent = []
    for n in range(PIECES):
        c, rows = piece(n)
        for which, (target, slot, head) in enumerate(
            ((device(1, 0), 2 + core, 0), (device(1, 1), 2 + core, 1), (partner, core, other))
        ):
            copy = remote(
                own[c].at[rows, head_cols(head)], kv.at[slot, c, rows],
                kv_send.at[which, n], kv_recv.at[slot, n], target,
            )
            copy.start()
            sent.append(copy)
    acts = []
    for n, (src, dst) in enumerate(((q_ref, q_nat), (do_ref, do_nat))):
        copy = remote(
            src.at[:, span_cols(other)], dst.at[core], act_send.at[n], act_recv.at[n], partner
        )
        copy.start()
        acts.append(copy)

    def arrived(slot, n):
        c, rows = piece(n)
        remote(
            kv.at[slot, c, rows], kv.at[slot, c, rows], kv_send.at[3, n], kv_recv.at[slot, n], partner
        ).wait_recv()

    for n in range(PIECES):
        arrived(other, n)
    for copy in acts:
        copy.wait_recv()
    turn_queries(other)
    turn_keys(other)

    def chip_pairs(t, carry):
        first = t == 0
        forward(jnp.where(first, other, 1), jnp.where(first, other, 0), jnp.where(first, 4 * other, 5))
        return carry

    lax.fori_loop(0, 2, chip_pairs, 0)

    for n in range(PIECES):
        arrived(3, n)
        c, rows = piece(n)
        copy = remote(
            kv.at[3, c, rows], kv.at[4, c, rows],
            kv_send.at[3, n], kv_recv.at[4, n], device(1, 0) + core,
        )
        copy.start()
        sent.append(copy)
    for n in range(PIECES):
        arrived(2, n)
    turn_keys(3)
    turn_keys(2)

    def before_pairs(t, carry):
        qs = lax.rem(t, 2)
        forward(qs, 3 - t // 2, 5 * qs + 1 + t // 2)
        return carry

    lax.fori_loop(0, 4, before_pairs, 0)
    outs = []

    def hand_out(stage, dst, n, qs):
        here = pltpu.make_async_copy(
            stage.at[qs], dst.at[:, span_cols(core)], local_sem.at[n]
        )
        there = remote(
            stage.at[qs], dst.at[:, span_cols(core)], out_send.at[n], out_recv.at[n], partner
        )

        @pl.when(core == qs)
        def _():
            here.start()

        @pl.when(core != qs)
        def _():
            there.start()

        if qs == 0:
            outs.append((here, there))

    def hand_gradient(slot):
        for n in range(PIECES):
            c, rows = piece(n)

            @pl.when(core != slot)
            def _():
                g_out[3, c, rows] = grad_piece(slot, n).astype(BF16)
                remote(
                    g_out.at[3, c, rows], g_near.at[c, rows], g_send.at[3, n], g_recv.at[3, n], partner
                ).start()

    finish_forward(1)
    hand_out(o_stage, o_ref, 0, 1)

    def odd_back(t, carry):
        backward(1, lax.rem(t + 2, 4), 7 - t)
        return carry

    lax.fori_loop(0, 4, odd_back, 0)
    finish_backward(1)
    hand_out(dq_stage, dq_ref, 1, 1)
    hand_gradient(1)

    for n in range(PIECES):
        arrived(4, n)
    turn_keys(4)
    forward(0, 4, 3)
    finish_forward(0)
    hand_out(o_stage, o_ref, 0, 0)

    def send_gradient(slot, which, n, dst, recv, target):
        c, rows = piece(n)
        remote(
            g_out.at[which, c, rows], dst.at[c, rows], g_send.at[which, n], recv, target
        ).start()

    def even_back(t, carry):
        slot = jnp.where(t == 0, 4, jnp.where(t == 3, 0, 4 - t))
        pair = jnp.where(t == 0, 3, jnp.where(t == 3, 0, t))
        backward(0, slot, pair)

        @pl.when(t == 0)
        def _():
            for n in range(PIECES):
                c, rows = piece(n)
                g_out[0, c, rows] = grad_piece(4, n).astype(BF16)
                send_gradient(4, 0, n, g_relay, g_recv.at[0, n], device(-1, 0) + core)

        @pl.when(t == 2)
        def _():
            for n in range(PIECES):
                c, rows = piece(n)
                g_out[1, c, rows] = grad_piece(2, n).astype(BF16)
                send_gradient(2, 1, n, g_far.at[core], g_recv.at[1 + core, n], device(-1, 0))

        return carry

    lax.fori_loop(0, 4, even_back, 0)
    hand_gradient(0)
    finish_backward(0)
    hand_out(dq_stage, dq_ref, 1, 0)

    for n in range(PIECES):
        c, rows = piece(n)
        remote(
            g_out.at[0, c, rows], g_relay.at[c, rows], g_send.at[0, n], g_recv.at[0, n], partner
        ).wait_recv()
        g_out[2, c, rows] = (grad_piece(3, n) + g_relay[c, rows].astype(F32)).astype(BF16)
        send_gradient(3, 2, n, g_far.at[core], g_recv.at[1 + core, n], device(-1, 1))

    for n in range(PIECES):
        c, rows = piece(n)
        remote(
            g_out.at[3, c, rows], g_near.at[c, rows], g_send.at[3, n], g_recv.at[3, n], partner
        ).wait_recv()
        for head in range(2):
            remote(
                g_out.at[1, c, rows], g_far.at[head, c, rows],
                g_send.at[1, n], g_recv.at[1 + head, n], partner,
            ).wait_recv()
        buf = (gk_buf, gv_buf)[c]
        mine = grad_piece(core, n) + g_far[core, c, rows].astype(F32)
        theirs = g_near[c, rows].astype(F32) + g_far[other, c, rows].astype(F32)
        buf[rows, head_cols(core)] = mine.astype(BF16)
        buf[rows, head_cols(other)] = theirs.astype(BF16)
    ends = [
        pltpu.make_async_copy(gk_buf, gk_ref, local_sem.at[2]),
        pltpu.make_async_copy(gv_buf, gv_ref, local_sem.at[3]),
    ]
    for copy in ends:
        copy.start()
    for copy in ends:
        copy.wait()
    for here, there in outs:
        here.wait()
        there.wait()
    for copy in sent + acts:
        copy.wait_send()
    for which in range(4):
        for n in range(PIECES):
            c, rows = piece(n)
            remote(
                g_out.at[which, c, rows], g_relay.at[c, rows],
                g_send.at[which, n], g_recv.at[0, n], partner,
            ).wait_send()


def per_device(queries, keys, values, output_gradient, lengths):
    count = lax.axis_size("ctx")
    width = KEY_VALUE_HEADS * HEAD
    wide = QUERY_HEADS * HEAD
    dma = pltpu.SemaphoreType.DMA
    vmem = pltpu.VMEM
    shapes = [
        jax.ShapeDtypeStruct((ROWS, wide), BF16),
        jax.ShapeDtypeStruct((ROWS, wide), BF16),
        jax.ShapeDtypeStruct((ROWS, width), BF16),
        jax.ShapeDtypeStruct((ROWS, width), BF16),
    ]
    return pl.pallas_call(
        functools.partial(fused_kernel, count),
        out_shape=shapes,
        in_specs=[SMEM] + [HBM] * 4,
        out_specs=[HBM] * 4,
        scratch_shapes=[
            vmem((SLOTS, 2, ROWS, HEAD), BF16),
            vmem((SLOTS, 2, HEAD, ROWS), BF16),
            vmem((2, ROWS, SPAN), BF16),
            vmem((2, ROWS, SPAN), BF16),
            vmem((2, GROUP, HEAD, ROWS), BF16),
            vmem((2, GROUP, HEAD, ROWS), BF16),
            vmem((8, ROWS, GROUP * ROWS), BF16),
            vmem((8, 8, ROWS), F32),
            vmem((2, 8, ROWS), F32),
            vmem((2, 8, ROWS), F32),
            vmem((2, GROUP, HEAD, ROWS), F32),
            vmem((2, GROUP, HEAD, ROWS), F32),
            vmem((2, 8, ROWS), F32),
            vmem((2, 8, ROWS), F32),
            vmem((2, 8, ROWS), jnp.int32),
            vmem((SLOTS, 2, ROWS, HEAD), F32),
            vmem((3, ROWS, ROWS), F32),
            vmem((ROWS, GROUP * ROWS), BF16),
            vmem((ROWS, GROUP * ROWS), BF16),
            vmem((ROWS, ROWS), F32),
            vmem((2, ROWS, SPAN), BF16),
            vmem((2, ROWS, SPAN), BF16),
            vmem((4, 2, ROWS, HEAD), BF16),
            vmem((2, ROWS, HEAD), BF16),
            vmem((2, 2, ROWS, HEAD), BF16),
            vmem((2, ROWS, HEAD), BF16),
            vmem((ROWS, width), BF16),
            vmem((ROWS, width), BF16),
            dma((4,)),
            dma((4, PIECES)),
            dma((SLOTS, PIECES)),
            dma((2,)),
            dma((2,)),
            dma((2,)),
            dma((2,)),
            dma((4, PIECES)),
            dma((4, PIECES)),
        ],
        compiler_params=pltpu.CompilerParams(
            collective_id=0, has_side_effects=True, vmem_limit_bytes=64 << 20
        ),
        name="attention",
    )(lengths, queries, keys, values, output_gradient)


def solution(mesh):
    split = P(("dp", "ctx"), None)
    return jax.shard_map(
        per_device,
        mesh=mesh,
        in_specs=(split, split, split, split, P("dp")),
        out_specs=(split, split, split, split),
        check_vma=False,
    )
```

```python
import functools
import math

import jax
import jax.numpy as jnp
from jax import lax
from jax.experimental import pallas as pl
from jax.experimental.pallas import tpu as pltpu
from jax.sharding import PartitionSpec as P

QUERY_HEADS = 14
KEY_VALUE_HEADS = 2
HEAD = 128
GROUP = QUERY_HEADS // KEY_VALUE_HEADS
SPAN = GROUP * HEAD
DOCS = 32
ROWS = 256
SLOTS = 5
LANES = GROUP * ROWS
EXTRA = 16
PIECES = 4
PIECE_ROWS = ROWS // 2
NEGATIVE_FILL = -1e30
SCALE = 1.0 / math.sqrt(HEAD)
LOG2E_SCALE = math.log2(math.e) * SCALE
BF16 = jnp.bfloat16
F32 = jnp.float32
MESH = pl.DeviceIdType.MESH
SMEM = pl.BlockSpec(memory_space=pltpu.SMEM)
HBM = pl.BlockSpec(memory_space=pltpu.HBM)
ANY = pl.BlockSpec(memory_space=pl.ANY)


def dot_nn(a, b):
    return lax.dot_general(a, b, (((1,), (0,)), ((), ())), preferred_element_type=F32)


def remote(src, dst, send, recv, target):
    return pltpu.make_async_remote_copy(
        src_ref=src, dst_ref=dst, send_sem=send, recv_sem=recv,
        device_id={"ctx": target}, device_id_type=MESH,
    )


def fused_kernel(
    count, len_ref, q_ref, k_ref, v_ref, do_ref,
    o_ref, dq_ref, gk_ref, gv_ref,
    kv, k_t, v_t, q_nat, do_nat, q_t, do_t, e_all, m_pair, shrink_buf, m_run, o_t, dq_t, delta, inv, starts,
    g_sum, s_buf, p_buf, ds_buf, bias, o_stage, dq_stage, g_out, g_relay, g_far, g_end,
    local_sem, end_sem, kv_send, kv_recv, act_local, act_send, act_recv, out_send, out_recv, g_send, g_recv,
):
    me = lax.axis_index("ctx")
    core = lax.rem(me, 2)
    other = 1 - core
    chip = me // 2
    partner = me + 1 - 2 * core

    ahead = lax.rem(me + 2, count)
    behind = lax.rem(me - 2 + count, count)

    def head_cols(which):
        return pl.ds(pl.multiple_of(which * HEAD, HEAD), HEAD)

    def span_cols(which):
        return pl.ds(pl.multiple_of(which * SPAN, HEAD), SPAN)

    def piece(n):
        return n // 2, pl.ds((n % 2) * PIECE_ROWS, PIECE_ROWS)

    def group_cols(which, h):
        return pl.ds(pl.multiple_of(which * SPAN + h * HEAD, HEAD), HEAD)

    def head_rows(h):
        return pl.ds(h * ROWS, ROWS)

    local = [
        pltpu.make_async_copy(k_ref.at[:, head_cols(core)], kv.at[core, 0], local_sem.at[2]),
        pltpu.make_async_copy(v_ref.at[:, head_cols(core)], kv.at[core, 1], local_sem.at[3]),
    ]
    for n, (src, dst) in enumerate(((q_ref, q_nat), (do_ref, do_nat))):
        for h in range(GROUP):
            local.append(
                pltpu.make_async_copy(
                    src.at[:, group_cols(core, h)], dst.at[core, head_rows(h)], act_local.at[n, h]
                )
            )
    for copy in local:
        copy.start()
    barrier = pltpu.get_barrier_semaphore()
    for target in (partner, ahead, behind):
        pl.semaphore_signal(barrier, inc=1, device_id={"ctx": target}, device_id_type=MESH)

    m_run[...] = jnp.full_like(m_run, NEGATIVE_FILL)
    o_t[...] = jnp.zeros_like(o_t)
    dq_t[...] = jnp.zeros_like(dq_t)
    g_sum[...] = jnp.zeros_like(g_sum)
    for qs in range(2):
        q_pos = (2 * chip + qs) * ROWS + lax.broadcasted_iota(jnp.int32, (8, ROWS), 1)
        start = jnp.zeros((8, ROWS), jnp.int32)
        total = jnp.int32(0)
        for d in range(DOCS):
            total = total + len_ref[d]
            start = jnp.where(q_pos >= total, total, start)
        starts[qs] = start

    def turn_queries(qs):
        for h in range(GROUP):
            lanes = slice(h * ROWS, (h + 1) * ROWS)
            q_t[qs, :, lanes] = q_nat[qs, h * ROWS : (h + 1) * ROWS].T
            do_t[qs, :, lanes] = do_nat[qs, h * ROWS : (h + 1) * ROWS].T

    def turn_keys(slot):
        k_t[slot] = kv[slot, 0].T
        v_t[slot, :HEAD] = kv[slot, 1].T
        v_t[slot, HEAD:] = jnp.ones((EXTRA, ROWS), BF16)

    def block_of(slot):
        return 2 * chip + jnp.where(slot < 2, slot, jnp.where(slot == 4, -3, slot - 4))

    def staged(stages, units):
        for step in range(len(units) + len(stages) - 1):
            for lag, stage in enumerate(stages):
                if 0 <= step - lag < len(units):
                    stage(step - lag, *units[step - lag])

    heads = [slice(h * ROWS, (h + 1) * ROWS) for h in range(GROUP)]

    def forward(units):

        def scores(place, qs, slot, pair):
            q_pos = (2 * chip + qs) * ROWS + lax.broadcasted_iota(jnp.int32, (1, ROWS), 1)
            k_pos = block_of(slot) * ROWS + lax.broadcasted_iota(jnp.int32, (ROWS, ROWS), 0)
            inside = (k_pos <= q_pos) & (k_pos >= starts[qs, 0:1])
            bias[place % 2] = jnp.where(inside, 0.0, NEGATIVE_FILL)
            s = dot_nn(kv[slot, 0], q_t[qs])
            for lanes in heads:
                masked = s[:, lanes] + bias[place % 2]
                s_buf[place % 2, :, lanes] = masked
                old = m_run[qs, 0:1, lanes]
                top = jnp.maximum(old, jnp.max(masked, axis=0, keepdims=True))
                m_run[qs, 0:1, lanes] = top
                m_pair[pair, 0:1, lanes] = top
                shrink_buf[place % 3, 0:1, lanes] = jnp.exp2((old - top) * LOG2E_SCALE)

        def soft(place, qs, slot, pair):
            for lanes in heads:
                top = m_pair[pair, 0:1, lanes]
                e = jnp.exp2((s_buf[place % 2, :, lanes] - top) * LOG2E_SCALE)
                e_all[pair, :, lanes] = e.astype(BF16)

        def out(place, qs, slot, pair):
            o_t[qs] = o_t[qs] * shrink_buf[place % 3, 0:1] + dot_nn(v_t[slot], e_all[pair])

        staged((scores, soft, out), units)

    def finish_forward(qs):
        for h, lanes in enumerate(heads):
            r = 1.0 / o_t[qs, HEAD : HEAD + 1, lanes]
            low = (o_t[qs, :HEAD, lanes] * r).astype(BF16)
            o_stage[qs, :, h * HEAD : (h + 1) * HEAD] = low.T
            inv[qs, 0:1, lanes] = r
            delta[qs, 0:1, lanes] = jnp.sum(
                do_t[qs, :, lanes].astype(F32) * low.astype(F32), axis=0, keepdims=True
            )

    def backward(units):
        def dprob(place, qs, slot, pair):
            s_buf[place % 2] = dot_nn(kv[slot, 1], do_t[qs])

        def dscore(place, qs, slot, pair):
            for lanes in heads:
                factor = jnp.exp2((m_pair[pair, 0:1, lanes] - m_run[qs, 0:1, lanes]) * LOG2E_SCALE)
                factor = factor * inv[qs, 0:1, lanes]
                p = e_all[pair, :, lanes].astype(F32) * factor
                p_buf[place % 2, :, lanes] = p.astype(BF16)
                ds_buf[place % 2, :, lanes] = (p * (s_buf[place % 2, :, lanes] - delta[qs, 0:1, lanes])).astype(
                    BF16
                )

        def grad(place, qs, slot, pair):
            g_sum[slot, 1] += dot_nn(p_buf[place % 2], do_nat[qs])
            g_sum[slot, 0] += dot_nn(ds_buf[place % 2], q_nat[qs])
            dq_t[qs] += dot_nn(k_t[slot], ds_buf[place % 2])

        staged((dprob, dscore, grad), units)

    def finish_backward(qs):
        for h, lanes in enumerate(heads):
            dq_stage[qs, :, h * HEAD : (h + 1) * HEAD] = (dq_t[qs, :, lanes] * SCALE).astype(BF16).T

    def grad_piece(slot, n):
        c, rows = piece(n)
        return g_sum[slot, c, rows] * (SCALE if c == 0 else 1.0)

    for copy in local:
        copy.wait()
    turn_queries(core)
    turn_keys(core)
    forward([(core, core, 4 * core)])
    pl.semaphore_wait(barrier, 3)

    own = (k_ref, v_ref)
    sent = []

    def send_kv(src, dst_slot, which, n, target):
        c, rows = piece(n)
        copy = remote(
            src, kv.at[dst_slot, c, rows], kv_send.at[which, n], kv_recv.at[dst_slot, n], target
        )
        copy.start()
        sent.append(copy)

    for n in range(PIECES):
        c, rows = piece(n)
        send_kv(kv.at[core, c, rows], 2 + core, 0, n, ahead)
    for n in range(PIECES):
        c, rows = piece(n)
        send_kv(own[c].at[rows, head_cols(other)], core, 1, n, partner)
    acts = []
    for n, (src, dst) in enumerate(((q_ref, q_nat), (do_ref, do_nat))):
        for h in range(GROUP):
            copy = remote(
                src.at[:, group_cols(other, h)], dst.at[core, head_rows(h)],
                act_send.at[n, h], act_recv.at[n, h], partner,
            )
            copy.start()
            acts.append(copy)

    def arrived(slot, n):
        c, rows = piece(n)
        remote(
            kv.at[slot, c, rows], kv.at[slot, c, rows], kv_send.at[3, n], kv_recv.at[slot, n], partner
        ).wait_recv()

    for n in range(PIECES):
        arrived(other, n)
        c, rows = piece(n)
        send_kv(kv.at[other, c, rows], 2 + other, 2, n, ahead)
    for copy in acts:
        copy.wait_recv()
    turn_queries(other)
    turn_keys(other)

    forward([(other, other, 4 * other), (1, 0, 5)])

    for n in range(PIECES):
        arrived(3, n)
        c, rows = piece(n)
        send_kv(kv.at[3, c, rows], 4, 3, n, ahead)
    for n in range(PIECES):
        arrived(2, n)
    turn_keys(3)
    turn_keys(2)

    forward([(1, 3, 6), (1, 2, 7), (0, 3, 1), (0, 2, 2)])
    outs = []

    def hand_out(stage, dst, n, qs):
        here = pltpu.make_async_copy(
            stage.at[qs], dst.at[:, span_cols(core)], local_sem.at[n]
        )
        there = remote(
            stage.at[qs], dst.at[:, span_cols(core)], out_send.at[n], out_recv.at[n], partner
        )

        @pl.when(core == qs)
        def _():
            here.start()

        @pl.when(core != qs)
        def _():
            there.start()

        if qs == 0:
            outs.append((here, there))

    def send_gradient(slot, which, dst, extra=None):
        for n in range(PIECES):
            c, rows = piece(n)
            value = grad_piece(slot, n)
            if extra is not None:
                remote(
                    g_out.at[0, c, rows], extra.at[c, rows], g_send.at[0, n], g_recv.at[0, n], partner
                ).wait_recv()
                value = value + extra[c, rows].astype(F32)
            g_out[which, c, rows] = value.astype(BF16)
            remote(
                g_out.at[which, c, rows], dst.at[c, rows],
                g_send.at[which, n], g_recv.at[which, n], behind,
            ).start()

    finish_forward(1)
    hand_out(o_stage, o_ref, 0, 1)
    backward([(1, 2, 7)])

    for n in range(PIECES):
        arrived(4, n)
    turn_keys(4)
    forward([(0, 4, 3)])
    finish_forward(0)
    hand_out(o_stage, o_ref, 0, 0)
    backward([(0, 4, 3)])
    send_gradient(4, 0, g_relay)
    backward([(0, 2, 2)])
    send_gradient(2, 1, g_far.at[0])
    backward([(1, 3, 6), (0, 3, 1), (1, 0, 5)])
    send_gradient(3, 2, g_far.at[1], g_relay)
    backward([(1, 1, 4), (0, 0, 0)])
    finish_backward(1)
    hand_out(dq_stage, dq_ref, 1, 1)
    finish_backward(0)
    hand_out(dq_stage, dq_ref, 1, 0)

    grads = (gk_ref, gv_ref)
    ends = []
    for slot in range(2):
        for n in range(PIECES):
            c, rows = piece(n)
            remote(
                g_out.at[1 + slot, c, rows], g_far.at[slot, c, rows],
                g_send.at[1 + slot, n], g_recv.at[1 + slot, n], partner,
            ).wait_recv()
            g_end[slot, c, rows] = (grad_piece(slot, n) + g_far[slot, c, rows].astype(F32)).astype(
                BF16
            )
            dst = grads[c].at[rows, head_cols(core)]
            here = pltpu.make_async_copy(g_end.at[slot, c, rows], dst, end_sem.at[n])
            there = remote(
                g_end.at[slot, c, rows], dst, g_send.at[3, n], g_recv.at[3, n], partner
            )

            @pl.when(core == slot)
            def _():
                here.start()

            @pl.when(core != slot)
            def _():
                there.start()

            if slot == 1:
                ends.append((here, there))
    for here, there in outs + ends:
        here.wait()
        there.wait()
    for copy in sent + acts:
        copy.wait_send()
    for which in range(3):
        for n in range(PIECES):
            c, rows = piece(n)
            remote(
                g_out.at[which, c, rows], g_relay.at[c, rows],
                g_send.at[which, n], g_recv.at[0, n], partner,
            ).wait_send()


def copy_kernel(*refs):
    half = len(refs) // 2
    copies = [
        pltpu.make_async_copy(refs[n], refs[half + n], refs[-1].at[n]) for n in range(half)
    ]
    for copy in copies:
        copy.start()
    for copy in copies:
        copy.wait()


def per_device(queries, keys, values, output_gradient, lengths):
    count = lax.axis_size("ctx")
    width = KEY_VALUE_HEADS * HEAD
    wide = QUERY_HEADS * HEAD
    operands = (lengths, queries, keys, values, output_gradient)
    dma = pltpu.SemaphoreType.DMA
    vmem = pltpu.VMEM
    shapes = [
        jax.ShapeDtypeStruct((ROWS, wide), BF16),
        jax.ShapeDtypeStruct((ROWS, wide), BF16),
        jax.ShapeDtypeStruct((ROWS, width), BF16),
        jax.ShapeDtypeStruct((ROWS, width), BF16),
    ]
    results = pl.pallas_call(
        functools.partial(fused_kernel, count),
        out_shape=shapes,
        in_specs=[SMEM] + [HBM] * 4,
        out_specs=[ANY] * 4,
        scratch_shapes=[
            vmem((SLOTS, 2, ROWS, HEAD), BF16),
            vmem((SLOTS, HEAD, ROWS), BF16),
            vmem((SLOTS, HEAD + EXTRA, ROWS), BF16),
            vmem((2, LANES, HEAD), BF16),
            vmem((2, LANES, HEAD), BF16),
            vmem((2, HEAD, LANES), BF16),
            vmem((2, HEAD, LANES), BF16),
            vmem((8, ROWS, LANES), BF16),
            vmem((8, 8, LANES), F32),
            vmem((3, 8, LANES), F32),
            vmem((2, 8, LANES), F32),
            vmem((2, HEAD + EXTRA, LANES), F32),
            vmem((2, HEAD, LANES), F32),
            vmem((2, 8, LANES), F32),
            vmem((2, 8, LANES), F32),
            vmem((2, 8, ROWS), jnp.int32),
            vmem((SLOTS, 2, ROWS, HEAD), F32),
            vmem((2, ROWS, LANES), F32),
            vmem((2, ROWS, LANES), BF16),
            vmem((2, ROWS, LANES), BF16),
            vmem((2, ROWS, ROWS), F32),
            vmem((2, ROWS, SPAN), BF16),
            vmem((2, ROWS, SPAN), BF16),
            vmem((3, 2, ROWS, HEAD), BF16),
            vmem((2, ROWS, HEAD), BF16),
            vmem((2, 2, ROWS, HEAD), BF16),
            vmem((2, 2, ROWS, HEAD), BF16),
            dma((4,)),
            dma((PIECES,)),
            dma((4, PIECES)),
            dma((SLOTS, PIECES)),
            dma((2, GROUP)),
            dma((2, GROUP)),
            dma((2, GROUP)),
            dma((2,)),
            dma((2,)),
            dma((4, PIECES)),
            dma((4, PIECES)),
        ],
        compiler_params=pltpu.CompilerParams(
            collective_id=0, has_side_effects=True, vmem_limit_bytes=48 << 20
        ),
        name="attention",
    )(*(pltpu.with_memory_space_constraint(x, pltpu.HBM) for x in operands))
    return pl.pallas_call(
        copy_kernel,
        out_shape=[pltpu.HBM(x.shape, x.dtype) for x in shapes],
        in_specs=[ANY] * 4,
        out_specs=[HBM] * 4,
        scratch_shapes=[dma((4,))],
        name="place_results",
    )(*(pltpu.with_memory_space_constraint(x, pltpu.VMEM) for x in results))


def solution(mesh):
    split = P(("dp", "ctx"), None)
    return jax.shard_map(
        per_device,
        mesh=mesh,
        in_specs=(split, split, split, split, P("dp")),
        out_specs=(split, split, split, split),
        check_vma=False,
    )
```

```python
import functools
import math

import jax
import jax.numpy as jnp
from jax import lax
from jax.experimental import pallas as pl
from jax.experimental.pallas import tpu as pltpu
from jax.sharding import PartitionSpec as P

QUERY_HEADS = 14
KEY_VALUE_HEADS = 2
HEAD = 128
GROUP = QUERY_HEADS // KEY_VALUE_HEADS
SPAN = GROUP * HEAD
DOCS = 32
ROWS = 256
SLOTS = 5
RUN = 4
LANES = GROUP * ROWS
EXTRA = 16
PIECES = 4
PIECE_ROWS = 2 * ROWS // PIECES
EARLY = PIECES // 2
NEGATIVE_FILL = -1e30
SCALE = 1.0 / math.sqrt(HEAD)
LOG2E_SCALE = math.log2(math.e) * SCALE
BF16 = jnp.bfloat16
F32 = jnp.float32
MESH = pl.DeviceIdType.MESH
SMEM = pl.BlockSpec(memory_space=pltpu.SMEM)
HBM = pl.BlockSpec(memory_space=pltpu.HBM)
ANY = pl.BlockSpec(memory_space=pl.ANY)


def dot_nn(a, b):
    return lax.dot_general(a, b, (((1,), (0,)), ((), ())), preferred_element_type=F32)


def remote(src, dst, send, recv, target):
    return pltpu.make_async_remote_copy(
        src_ref=src, dst_ref=dst, send_sem=send, recv_sem=recv,
        device_id={"ctx": target}, device_id_type=MESH,
    )


def fused_kernel(
    count, len_ref, q_ref, k_ref, v_ref, do_ref,
    o_ref, dq_ref, gk_ref, gv_ref,
    kv, k_t, v_t, q_nat, do_nat, q_t, do_t, e_all, m_pair, shrink_buf, m_run, o_t, dq_t, delta, inv, starts,
    g_sum, s_buf, p_buf, ds_buf, bias, o_stage, dq_stage, g_out, g_relay, g_direct, g_far, g_end,
    local_sem, end_sem, kv_send, kv_recv, act_local, act_send, act_recv, out_send, out_recv, g_send, g_recv,
):
    me = lax.axis_index("ctx")
    core = lax.rem(me, 2)
    other = 1 - core
    chip = me // 2
    partner = me + 1 - 2 * core

    ahead = lax.rem(me + 2, count)
    behind = lax.rem(me - 2 + count, count)

    def head_cols(which):
        return pl.ds(pl.multiple_of(which * HEAD, HEAD), HEAD)

    def span_cols(which):
        return pl.ds(pl.multiple_of(which * SPAN, HEAD), SPAN)

    def piece(n):
        half = PIECES // 2
        return n // half, pl.ds((n % half) * PIECE_ROWS, PIECE_ROWS)

    def group_cols(which, h):
        return pl.ds(pl.multiple_of(which * SPAN + h * HEAD, HEAD), HEAD)

    def head_rows(h):
        return pl.ds(h * ROWS, ROWS)

    local = [
        pltpu.make_async_copy(k_ref.at[:, head_cols(core)], kv.at[core, 0], local_sem.at[2]),
        pltpu.make_async_copy(v_ref.at[:, head_cols(core)], kv.at[core, 1], local_sem.at[3]),
    ]
    for n, (src, dst) in enumerate(((q_ref, q_nat), (do_ref, do_nat))):
        for h in range(GROUP):
            local.append(
                pltpu.make_async_copy(
                    src.at[:, group_cols(core, h)], dst.at[core, head_rows(h)], act_local.at[n, h]
                )
            )
    for copy in local:
        copy.start()
    barrier = pltpu.get_barrier_semaphore()
    has_next = chip < count // 2 - 1
    has_prev = chip > 0
    place_in_run = lax.rem(chip, RUN)
    far_next = (place_in_run == RUN - 2) & (chip + 2 < count // 2)
    far_prev = (place_in_run == 0) & (chip >= 2)
    passes_on = has_next & (place_in_run != RUN - 1)
    far_ahead = lax.rem(me + 4, count)
    far_behind = lax.rem(me - 4 + count, count)

    def greet(target):
        pl.semaphore_signal(barrier, inc=1, device_id={"ctx": target}, device_id_type=MESH)

    greet(partner)

    @pl.when(has_next)
    def _():
        greet(ahead)

    @pl.when(has_prev)
    def _():
        greet(behind)

    @pl.when(far_next)
    def _():
        greet(far_ahead)

    @pl.when(far_prev)
    def _():
        greet(far_behind)

    @pl.when(chip == 0)
    def _():
        kv[2:] = jnp.zeros((SLOTS - 2, 2, ROWS, HEAD), BF16)

    @pl.when(chip == count // 2 - 1)
    def _():
        g_far[...] = jnp.zeros_like(g_far)

    @pl.when(jnp.logical_not(passes_on))
    def _():
        g_relay[...] = jnp.zeros_like(g_relay)

    @pl.when(jnp.logical_not(far_next))
    def _():
        g_direct[...] = jnp.zeros_like(g_direct)

    m_run[...] = jnp.full_like(m_run, NEGATIVE_FILL)
    o_t[...] = jnp.zeros_like(o_t)
    dq_t[...] = jnp.zeros_like(dq_t)
    g_sum[...] = jnp.zeros_like(g_sum)
    for qs in range(2):
        q_pos = (2 * chip + qs) * ROWS + lax.broadcasted_iota(jnp.int32, (8, ROWS), 1)
        start = jnp.zeros((8, ROWS), jnp.int32)
        total = jnp.int32(0)
        for d in range(DOCS):
            total = total + len_ref[d]
            start = jnp.where(q_pos >= total, total, start)
        starts[qs] = start

    def turn_queries(qs):
        for h in range(GROUP):
            lanes = slice(h * ROWS, (h + 1) * ROWS)
            q_t[qs, :, lanes] = q_nat[qs, h * ROWS : (h + 1) * ROWS].T
            do_t[qs, :, lanes] = do_nat[qs, h * ROWS : (h + 1) * ROWS].T

    def turn_keys(slot, which=(0, 1)):
        if 0 in which:
            k_t[slot] = kv[slot, 0].T
        if 1 in which:
            v_t[slot, :HEAD] = kv[slot, 1].T
            v_t[slot, HEAD:] = jnp.ones((EXTRA, ROWS), BF16)

    def block_of(slot):
        return 2 * chip + jnp.where(slot < 2, slot, jnp.where(slot == 4, -3, slot - 4))

    def staged(stages, units):
        for step in range(len(units) + len(stages) - 1):
            for lag, stage in enumerate(stages):
                if 0 <= step - lag < len(units):
                    stage(step - lag, *units[step - lag])

    heads = [slice(h * ROWS, (h + 1) * ROWS) for h in range(GROUP)]

    def forward(units, before_out=None):

        def scores(place, qs, slot, pair):
            q_pos = (2 * chip + qs) * ROWS + lax.broadcasted_iota(jnp.int32, (1, ROWS), 1)
            k_pos = block_of(slot) * ROWS + lax.broadcasted_iota(jnp.int32, (ROWS, ROWS), 0)
            inside = (k_pos <= q_pos) & (k_pos >= starts[qs, 0:1])
            bias[place % 2] = jnp.where(inside, 0.0, NEGATIVE_FILL)
            s = dot_nn(kv[slot, 0], q_t[qs])
            for lanes in heads:
                masked = s[:, lanes] + bias[place % 2]
                s_buf[place % 2, :, lanes] = masked
                old = m_run[qs, 0:1, lanes]
                top = jnp.maximum(old, jnp.max(masked, axis=0, keepdims=True))
                m_run[qs, 0:1, lanes] = top
                m_pair[pair, 0:1, lanes] = top
                shrink_buf[place % 3, 0:1, lanes] = jnp.exp2((old - top) * LOG2E_SCALE)

        def soft(place, qs, slot, pair):
            for lanes in heads:
                top = m_pair[pair, 0:1, lanes]
                e = jnp.exp2((s_buf[place % 2, :, lanes] - top) * LOG2E_SCALE)
                e_all[pair, :, lanes] = e.astype(BF16)

        def out(place, qs, slot, pair):
            o_t[qs] = o_t[qs] * shrink_buf[place % 3, 0:1] + dot_nn(v_t[slot], e_all[pair])

        if before_out is None:
            staged((scores, soft, out), units)
        else:
            staged((scores, soft), units)
            before_out()
            staged((out,), units)

    def finish_forward(qs):
        for h, lanes in enumerate(heads):
            r = 1.0 / o_t[qs, HEAD : HEAD + 1, lanes]
            low = (o_t[qs, :HEAD, lanes] * r).astype(BF16)
            o_stage[qs, :, h * HEAD : (h + 1) * HEAD] = low.T
            inv[qs, 0:1, lanes] = r
            delta[qs, 0:1, lanes] = jnp.sum(
                do_t[qs, :, lanes].astype(F32) * low.astype(F32), axis=0, keepdims=True
            )

    def backward(units, between=None, after=None):
        def dprob(place, qs, slot, pair):
            s_buf[place % 2] = dot_nn(kv[slot, 1], do_t[qs])

        def dscore(place, qs, slot, pair):
            for lanes in heads:
                factor = jnp.exp2((m_pair[pair, 0:1, lanes] - m_run[qs, 0:1, lanes]) * LOG2E_SCALE)
                factor = factor * inv[qs, 0:1, lanes]
                p = e_all[pair, :, lanes].astype(F32) * factor
                p_buf[place % 2, :, lanes] = p.astype(BF16)
                ds_buf[place % 2, :, lanes] = (p * (s_buf[place % 2, :, lanes] - delta[qs, 0:1, lanes])).astype(
                    BF16
                )

        def grad(place, qs, slot, pair):
            g_sum[slot, 1] += dot_nn(p_buf[place % 2], do_nat[qs])
            if between is not None:
                between()
            g_sum[slot, 0] += dot_nn(ds_buf[place % 2], q_nat[qs])
            if after is not None:
                after()
            dq_t[qs] += dot_nn(k_t[slot], ds_buf[place % 2])

        staged((dprob, dscore, grad), units)

    def finish_backward(qs):
        for h, lanes in enumerate(heads):
            dq_stage[qs, :, h * HEAD : (h + 1) * HEAD] = (dq_t[qs, :, lanes] * SCALE).astype(BF16).T

    def grad_piece(slot, n):
        c, rows = piece(n)
        return g_sum[slot, c, rows] * (SCALE if c == 0 else 1.0)

    for copy in local:
        copy.wait()
    turn_queries(core)
    turn_keys(core)
    forward([(core, core, 4 * core)])
    greeted = 1
    for flag in (has_next, has_prev, far_next, far_prev):
        greeted = greeted + flag.astype(jnp.int32)
    pl.semaphore_wait(barrier, greeted)

    own = (k_ref, v_ref)
    sent = []

    def send_kv(src, dst_slot, which, n, target):
        c, rows = piece(n)
        copy = remote(
            src, kv.at[dst_slot, c, rows], kv_send.at[which, n], kv_recv.at[dst_slot, n], target
        )
        copy.start()
        return copy

    def send_own(n):
        c, rows = piece(n)
        send_kv(kv.at[core, c, rows], 2 + core, 0, n, ahead)

    def send_other(n):
        c, rows = piece(n)
        send_kv(kv.at[other, c, rows], 2 + other, 2, n, ahead)

    for n in range(PIECES):
        c, rows = piece(n)
        sent.append(send_kv(own[c].at[rows, head_cols(other)], core, 1, n, partner))

    early = jnp.where(core == 1, PIECES, EARLY)
    for n in range(PIECES):

        @pl.when(has_next & (n < early))
        def _():
            send_own(n)

    acts = []
    for n, (src, dst) in enumerate(((q_ref, q_nat), (do_ref, do_nat))):
        for h in range(GROUP):
            copy = remote(
                src.at[:, group_cols(other, h)], dst.at[core, head_rows(h)],
                act_send.at[n, h], act_recv.at[n, h], partner,
            )
            copy.start()
            acts.append(copy)

    def arrived(slot, n):
        c, rows = piece(n)
        copy = remote(
            kv.at[slot, c, rows], kv.at[slot, c, rows], kv_send.at[3, n], kv_recv.at[slot, n], partner
        )
        if isinstance(slot, int):

            @pl.when(has_prev)
            def _():
                copy.wait_recv()

        else:
            copy.wait_recv()

    for n in range(PIECES):
        arrived(other, n)

        @pl.when(has_next)
        def _():
            send_other(n)

    for n in range(EARLY, PIECES):

        @pl.when(has_next & (core == 0))
        def _():
            send_own(n)

    for n in range(PIECES):

        @pl.when(far_next)
        def _():
            c, rows = piece(n)
            send_kv(kv.at[1, c, rows], 4, 4, n, far_ahead)

    for copy in acts:
        copy.wait_recv()
    turn_queries(other)
    turn_keys(other)

    forward([(other, other, 4 * other), (1, 0, 5)])

    for n in range(PIECES):
        arrived(3, n)

        @pl.when(passes_on)
        def _():
            c, rows = piece(n)
            send_kv(kv.at[3, c, rows], 4, 3, n, ahead)

    for n in range(PIECES):
        arrived(2, n)
    turn_keys(3)
    turn_keys(2)

    forward([(1, 3, 6), (1, 2, 7), (0, 3, 1), (0, 2, 2)])
    outs = []

    def hand_out(stage, dst, n, qs):
        here = pltpu.make_async_copy(
            stage.at[qs], dst.at[:, span_cols(core)], local_sem.at[n]
        )
        there = remote(
            stage.at[qs], dst.at[:, span_cols(core)], out_send.at[n], out_recv.at[n], partner
        )

        @pl.when(core == qs)
        def _():
            here.start()

        @pl.when(core != qs)
        def _():
            there.start()

        if qs == 0:
            outs.append((here, there))

    def send_gradient(slot, which, dst, extra=None, pieces=range(PIECES)):
        for n in pieces:
            c, rows = piece(n)
            value = grad_piece(slot, n)
            if extra is not None:

                @pl.when(passes_on)
                def _():
                    remote(
                        g_out.at[0, c, rows], extra.at[c, rows],
                        g_send.at[0, n], g_recv.at[0, n], partner,
                    ).wait_recv()

                value = value + extra[c, rows].astype(F32)
            g_out[which, c, rows] = value.astype(BF16)

            near = has_prev
            if which == 0:
                near = has_prev & (place_in_run > 0)

                @pl.when(far_prev)
                def _():
                    remote(
                        g_out.at[which, c, rows], g_direct.at[c, rows],
                        g_send.at[which, n], g_recv.at[4, n], far_behind,
                    ).start()

            @pl.when(near)
            def _():
                remote(
                    g_out.at[which, c, rows], dst.at[c, rows],
                    g_send.at[which, n], g_recv.at[which, n], behind,
                ).start()

    finish_forward(1)
    hand_out(o_stage, o_ref, 0, 1)
    for n in range(PIECES // 2):
        arrived(4, n)

    def last_values():
        for n in range(PIECES // 2, PIECES):
            arrived(4, n)
        turn_keys(4)

    forward([(0, 4, 3)], last_values)
    finish_forward(0)
    hand_out(o_stage, o_ref, 0, 0)
    halves = (range(PIECES // 2), range(PIECES // 2, PIECES))
    backward(
        [(0, 4, 3)],
        lambda: send_gradient(4, 0, g_relay, pieces=halves[1]),
        lambda: send_gradient(4, 0, g_relay, pieces=halves[0]),
    )
    backward([(1, 2, 7), (0, 2, 2)])
    send_gradient(2, 1, g_far.at[0])
    backward([(1, 3, 6), (0, 3, 1)])
    send_gradient(3, 2, g_far.at[1], g_relay)
    backward([(1, 0, 5), (1, 1, 4), (0, 0, 0)])
    finish_backward(1)
    hand_out(dq_stage, dq_ref, 1, 1)
    finish_backward(0)
    hand_out(dq_stage, dq_ref, 1, 0)

    grads = (gk_ref, gv_ref)
    ends = []
    for slot in range(2):
        for n in range(PIECES):
            c, rows = piece(n)

            @pl.when(has_next)
            def _():
                remote(
                    g_out.at[1 + slot, c, rows], g_far.at[slot, c, rows],
                    g_send.at[1 + slot, n], g_recv.at[1 + slot, n], partner,
                ).wait_recv()

            value = grad_piece(slot, n) + g_far[slot, c, rows].astype(F32)
            if slot == 1:

                @pl.when(far_next)
                def _():
                    remote(
                        g_out.at[0, c, rows], g_direct.at[c, rows],
                        g_send.at[0, n], g_recv.at[4, n], partner,
                    ).wait_recv()

                value = value + g_direct[c, rows].astype(F32)
            g_end[slot, c, rows] = value.astype(BF16)
            dst = grads[c].at[rows, head_cols(core)]
            here = pltpu.make_async_copy(g_end.at[slot, c, rows], dst, end_sem.at[n])
            there = remote(
                g_end.at[slot, c, rows], dst, g_send.at[3, n], g_recv.at[3, n], partner
            )

            @pl.when(core == slot)
            def _():
                here.start()

            @pl.when(core != slot)
            def _():
                there.start()

            if slot == 1:
                ends.append((here, there))
    for here, there in outs + ends:
        here.wait()
        there.wait()
    for copy in sent + acts:
        copy.wait_send()
    for n in range(PIECES):
        c, rows = piece(n)

        def gone(which):
            remote(
                kv.at[0, c, rows], kv.at[0, c, rows],
                kv_send.at[which, n], kv_recv.at[0, n], partner,
            ).wait_send()

        def gone_gradient(which):
            remote(
                g_out.at[which, c, rows], g_relay.at[c, rows],
                g_send.at[which, n], g_recv.at[0, n], partner,
            ).wait_send()

        @pl.when(has_next)
        def _():
            gone(0)
            gone(2)

        @pl.when(passes_on)
        def _():
            gone(3)

        @pl.when(far_next)
        def _():
            gone(4)

        @pl.when(has_prev)
        def _():
            for which in range(3):
                gone_gradient(which)


def copy_kernel(*refs):
    half = len(refs) // 2
    copies = [
        pltpu.make_async_copy(refs[n], refs[half + n], refs[-1].at[n]) for n in range(half)
    ]
    for copy in copies:
        copy.start()
    for copy in copies:
        copy.wait()


def per_device(queries, keys, values, output_gradient, lengths):
    count = lax.axis_size("ctx")
    width = KEY_VALUE_HEADS * HEAD
    wide = QUERY_HEADS * HEAD
    operands = (lengths, queries, keys, values, output_gradient)
    dma = pltpu.SemaphoreType.DMA
    vmem = pltpu.VMEM
    shapes = [
        jax.ShapeDtypeStruct((ROWS, wide), BF16),
        jax.ShapeDtypeStruct((ROWS, wide), BF16),
        jax.ShapeDtypeStruct((ROWS, width), BF16),
        jax.ShapeDtypeStruct((ROWS, width), BF16),
    ]
    results = pl.pallas_call(
        functools.partial(fused_kernel, count),
        out_shape=shapes,
        in_specs=[SMEM] + [HBM] * 4,
        out_specs=[ANY] * 4,
        scratch_shapes=[
            vmem((SLOTS, 2, ROWS, HEAD), BF16),
            vmem((SLOTS, HEAD, ROWS), BF16),
            vmem((SLOTS, HEAD + EXTRA, ROWS), BF16),
            vmem((2, LANES, HEAD), BF16),
            vmem((2, LANES, HEAD), BF16),
            vmem((2, HEAD, LANES), BF16),
            vmem((2, HEAD, LANES), BF16),
            vmem((8, ROWS, LANES), BF16),
            vmem((8, 8, LANES), F32),
            vmem((3, 8, LANES), F32),
            vmem((2, 8, LANES), F32),
            vmem((2, HEAD + EXTRA, LANES), F32),
            vmem((2, HEAD, LANES), F32),
            vmem((2, 8, LANES), F32),
            vmem((2, 8, LANES), F32),
            vmem((2, 8, ROWS), jnp.int32),
            vmem((SLOTS, 2, ROWS, HEAD), F32),
            vmem((2, ROWS, LANES), F32),
            vmem((2, ROWS, LANES), BF16),
            vmem((2, ROWS, LANES), BF16),
            vmem((2, ROWS, ROWS), F32),
            vmem((2, ROWS, SPAN), BF16),
            vmem((2, ROWS, SPAN), BF16),
            vmem((3, 2, ROWS, HEAD), BF16),
            vmem((2, ROWS, HEAD), BF16),
            vmem((2, ROWS, HEAD), BF16),
            vmem((2, 2, ROWS, HEAD), BF16),
            vmem((2, 2, ROWS, HEAD), BF16),
            dma((4,)),
            dma((PIECES,)),
            dma((5, PIECES)),
            dma((SLOTS, PIECES)),
            dma((2, GROUP)),
            dma((2, GROUP)),
            dma((2, GROUP)),
            dma((2,)),
            dma((2,)),
            dma((4, PIECES)),
            dma((5, PIECES)),
        ],
        compiler_params=pltpu.CompilerParams(
            collective_id=0, has_side_effects=True, vmem_limit_bytes=48 << 20
        ),
        name="attention",
    )(*(pltpu.with_memory_space_constraint(x, pltpu.HBM) for x in operands))
    return pl.pallas_call(
        copy_kernel,
        out_shape=[pltpu.HBM(x.shape, x.dtype) for x in shapes],
        in_specs=[ANY] * 4,
        out_specs=[HBM] * 4,
        scratch_shapes=[dma((4,))],
        name="place_results",
    )(*(pltpu.with_memory_space_constraint(x, pltpu.VMEM) for x in results))


def solution(mesh):
    split = P(("dp", "ctx"), None)
    return jax.shard_map(
        per_device,
        mesh=mesh,
        in_specs=(split, split, split, split, P("dp")),
        out_specs=(split, split, split, split),
        check_vma=False,
    )
```

```python
import functools
import math

import jax
import jax.numpy as jnp
from jax import lax
from jax.experimental import pallas as pl
from jax.experimental.pallas import tpu as pltpu
from jax.sharding import PartitionSpec as P

QUERY_HEADS = 14
KEY_VALUE_HEADS = 2
HEAD = 128
GROUP = QUERY_HEADS // KEY_VALUE_HEADS
SPAN = GROUP * HEAD
DOCS = 32
ROWS = 256
SLOTS = 5
RUN = 4
LANES = GROUP * ROWS
EXTRA = 16
PIECES = 4
PIECE_ROWS = 2 * ROWS // PIECES
EARLY = PIECES // 2
NEGATIVE_FILL = -1e30
SCALE = 1.0 / math.sqrt(HEAD)
LOG2E_SCALE = math.log2(math.e) * SCALE
BF16 = jnp.bfloat16
F32 = jnp.float32
MESH = pl.DeviceIdType.MESH
SMEM = pl.BlockSpec(memory_space=pltpu.SMEM)
HBM = pl.BlockSpec(memory_space=pltpu.HBM)
ANY = pl.BlockSpec(memory_space=pl.ANY)


def dot_nn(a, b):
    return lax.dot_general(a, b, (((1,), (0,)), ((), ())), preferred_element_type=F32)


def remote(src, dst, send, recv, target):
    return pltpu.make_async_remote_copy(
        src_ref=src, dst_ref=dst, send_sem=send, recv_sem=recv,
        device_id={"ctx": target}, device_id_type=MESH,
    )


def fused_kernel(
    count, len_ref, q_ref, k_ref, v_ref, do_ref,
    o_ref, dq_ref, gk_ref, gv_ref,
    kv, k_t, v_t, q_nat, do_nat, q_t, do_t, e_all, m_pair, shrink_buf, m_run, o_t, dq_t, delta, inv, starts,
    g_sum, s_buf, p_buf, ds_buf, bias, o_stage, dq_stage, g_out, g_relay, g_direct, g_far, g_end,
    local_sem, end_sem, kv_send, kv_recv, act_local, act_send, act_recv, out_send, out_recv, g_send, g_recv,
):
    me = lax.axis_index("ctx")
    core = lax.rem(me, 2)
    other = 1 - core
    chip = me // 2
    partner = me + 1 - 2 * core

    ahead = lax.rem(me + 2, count)
    behind = lax.rem(me - 2 + count, count)

    def head_cols(which):
        return pl.ds(pl.multiple_of(which * HEAD, HEAD), HEAD)

    def span_cols(which):
        return pl.ds(pl.multiple_of(which * SPAN, HEAD), SPAN)

    def piece(n):
        half = PIECES // 2
        return n // half, pl.ds((n % half) * PIECE_ROWS, PIECE_ROWS)

    def group_cols(which, h):
        return pl.ds(pl.multiple_of(which * SPAN + h * HEAD, HEAD), HEAD)

    def head_rows(h):
        return pl.ds(h * ROWS, ROWS)

    local = [
        pltpu.make_async_copy(k_ref.at[:, head_cols(core)], kv.at[core, 0], local_sem.at[2]),
        pltpu.make_async_copy(v_ref.at[:, head_cols(core)], kv.at[core, 1], local_sem.at[3]),
    ]
    for n, (src, dst) in enumerate(((q_ref, q_nat), (do_ref, do_nat))):
        for h in range(GROUP):
            local.append(
                pltpu.make_async_copy(
                    src.at[:, group_cols(core, h)], dst.at[core, head_rows(h)], act_local.at[n, h]
                )
            )
    for copy in local:
        copy.start()
    barrier = pltpu.get_barrier_semaphore()
    has_next = chip < count // 2 - 1
    has_prev = chip > 0
    place_in_run = lax.rem(chip, RUN)
    far_next = (place_in_run == RUN - 2) & (chip + 2 < count // 2)
    far_prev = (place_in_run == 0) & (chip >= 2)
    passes_on = has_next & (place_in_run != RUN - 1)
    far_ahead = lax.rem(me + 4, count)
    far_behind = lax.rem(me - 4 + count, count)

    def greet(target):
        pl.semaphore_signal(barrier, inc=1, device_id={"ctx": target}, device_id_type=MESH)

    greet(partner)

    @pl.when(has_next)
    def _():
        greet(ahead)

    @pl.when(has_prev)
    def _():
        greet(behind)

    @pl.when(far_next)
    def _():
        greet(far_ahead)

    @pl.when(far_prev)
    def _():
        greet(far_behind)

    @pl.when(chip == 0)
    def _():
        kv[2:] = jnp.zeros((SLOTS - 2, 2, ROWS, HEAD), BF16)

    @pl.when(chip == count // 2 - 1)
    def _():
        g_far[...] = jnp.zeros_like(g_far)

    @pl.when(jnp.logical_not(passes_on))
    def _():
        g_relay[...] = jnp.zeros_like(g_relay)

    @pl.when(jnp.logical_not(far_next))
    def _():
        g_direct[...] = jnp.zeros_like(g_direct)

    m_run[...] = jnp.full_like(m_run, NEGATIVE_FILL)
    o_t[...] = jnp.zeros_like(o_t)
    dq_t[...] = jnp.zeros_like(dq_t)
    g_sum[...] = jnp.zeros_like(g_sum)
    for qs in range(2):
        q_pos = (2 * chip + qs) * ROWS + lax.broadcasted_iota(jnp.int32, (8, ROWS), 1)
        start = jnp.zeros((8, ROWS), jnp.int32)
        total = jnp.int32(0)
        for d in range(DOCS):
            total = total + len_ref[d]
            start = jnp.where(q_pos >= total, total, start)
        starts[qs] = start

    def turn_queries(qs):
        for h in range(GROUP):
            lanes = slice(h * ROWS, (h + 1) * ROWS)
            q_t[qs, :, lanes] = q_nat[qs, h * ROWS : (h + 1) * ROWS].T
            do_t[qs, :, lanes] = do_nat[qs, h * ROWS : (h + 1) * ROWS].T

    def turn_keys(slot, which=(0, 1)):
        if 0 in which:
            k_t[slot] = kv[slot, 0].T
        if 1 in which:
            v_t[slot, :HEAD] = kv[slot, 1].T
            v_t[slot, HEAD:] = jnp.ones((EXTRA, ROWS), BF16)

    def block_of(slot):
        return 2 * chip + jnp.where(slot < 2, slot, jnp.where(slot == 4, -3, slot - 4))

    def staged(stages, units):
        for step in range(len(units) + len(stages) - 1):
            for lag, stage in enumerate(stages):
                if 0 <= step - lag < len(units):
                    stage(step - lag, *units[step - lag])

    heads = [slice(h * ROWS, (h + 1) * ROWS) for h in range(GROUP)]

    def forward(units, before_out=None):

        def scores(place, qs, slot, pair):
            q_pos = (2 * chip + qs) * ROWS + lax.broadcasted_iota(jnp.int32, (1, ROWS), 1)
            k_pos = block_of(slot) * ROWS + lax.broadcasted_iota(jnp.int32, (ROWS, ROWS), 0)
            inside = (k_pos <= q_pos) & (k_pos >= starts[qs, 0:1])
            bias[place % 2] = jnp.where(inside, 0.0, NEGATIVE_FILL)
            s = dot_nn(kv[slot, 0], q_t[qs])
            for lanes in heads:
                masked = s[:, lanes] + bias[place % 2]
                s_buf[place % 2, :, lanes] = masked
                old = m_run[qs, 0:1, lanes]
                top = jnp.maximum(old, jnp.max(masked, axis=0, keepdims=True))
                m_run[qs, 0:1, lanes] = top
                m_pair[pair, 0:1, lanes] = top
                shrink_buf[place % 3, 0:1, lanes] = jnp.exp2((old - top) * LOG2E_SCALE)

        def soft(place, qs, slot, pair):
            for lanes in heads:
                top = m_pair[pair, 0:1, lanes]
                e = jnp.exp2((s_buf[place % 2, :, lanes] - top) * LOG2E_SCALE)
                e_all[pair, :, lanes] = e.astype(BF16)

        def out(place, qs, slot, pair):
            o_t[qs] = o_t[qs] * shrink_buf[place % 3, 0:1] + dot_nn(v_t[slot], e_all[pair])

        if before_out is None:
            staged((scores, soft, out), units)
        else:
            staged((scores, soft), units)
            before_out()
            staged((out,), units)

    def finish_forward(qs):
        for h, lanes in enumerate(heads):
            r = 1.0 / o_t[qs, HEAD : HEAD + 1, lanes]
            low = (o_t[qs, :HEAD, lanes] * r).astype(BF16)
            o_stage[qs, :, h * HEAD : (h + 1) * HEAD] = low.T
            inv[qs, 0:1, lanes] = r
            delta[qs, 0:1, lanes] = jnp.sum(
                do_t[qs, :, lanes].astype(F32) * low.astype(F32), axis=0, keepdims=True
            )

    def backward(units, between=None, after=None):
        def dprob(place, qs, slot, pair):
            s_buf[place % 2] = dot_nn(kv[slot, 1], do_t[qs])

        def dscore(place, qs, slot, pair):
            for lanes in heads:
                factor = jnp.exp2((m_pair[pair, 0:1, lanes] - m_run[qs, 0:1, lanes]) * LOG2E_SCALE)
                factor = factor * inv[qs, 0:1, lanes]
                p = e_all[pair, :, lanes].astype(F32) * factor
                p_buf[place % 2, :, lanes] = p.astype(BF16)
                ds_buf[place % 2, :, lanes] = (p * (s_buf[place % 2, :, lanes] - delta[qs, 0:1, lanes])).astype(
                    BF16
                )

        def grad(place, qs, slot, pair):
            g_sum[slot, 1] += dot_nn(p_buf[place % 2], do_nat[qs])
            if between is not None:
                between()
            g_sum[slot, 0] += dot_nn(ds_buf[place % 2], q_nat[qs])
            if after is not None:
                after()
            dq_t[qs] += dot_nn(k_t[slot], ds_buf[place % 2])

        staged((dprob, dscore, grad), units)

    def finish_backward(qs):
        for h, lanes in enumerate(heads):
            dq_stage[qs, :, h * HEAD : (h + 1) * HEAD] = (dq_t[qs, :, lanes] * SCALE).astype(BF16).T

    def grad_piece(slot, n):
        c, rows = piece(n)
        return g_sum[slot, c, rows] * (SCALE if c == 0 else 1.0)

    for copy in local:
        copy.wait()
    turn_queries(core)
    turn_keys(core)
    forward([(core, core, 4 * core)])
    greeted = 1
    for flag in (has_next, has_prev, far_next, far_prev):
        greeted = greeted + flag.astype(jnp.int32)
    pl.semaphore_wait(barrier, greeted)

    own = (k_ref, v_ref)
    sent = []

    def send_kv(src, dst_slot, which, n, target):
        c, rows = piece(n)
        copy = remote(
            src, kv.at[dst_slot, c, rows], kv_send.at[which, n], kv_recv.at[dst_slot, n], target
        )
        copy.start()
        return copy

    def send_own(n):
        c, rows = piece(n)
        send_kv(kv.at[core, c, rows], 2 + core, 0, n, ahead)

    def send_other(n):
        c, rows = piece(n)
        send_kv(kv.at[other, c, rows], 2 + other, 2, n, ahead)

    for n in range(PIECES):
        c, rows = piece(n)
        sent.append(send_kv(own[c].at[rows, head_cols(other)], core, 1, n, partner))

    early = jnp.where(core == 1, PIECES, EARLY)
    for n in range(PIECES):

        @pl.when(has_next & (n < early))
        def _():
            send_own(n)

    acts = []
    for n, (src, dst) in enumerate(((q_ref, q_nat), (do_ref, do_nat))):
        for h in range(GROUP):
            copy = remote(
                src.at[:, group_cols(other, h)], dst.at[core, head_rows(h)],
                act_send.at[n, h], act_recv.at[n, h], partner,
            )
            copy.start()
            acts.append(copy)

    def arrived(slot, n):
        c, rows = piece(n)
        copy = remote(
            kv.at[slot, c, rows], kv.at[slot, c, rows], kv_send.at[3, n], kv_recv.at[slot, n], partner
        )
        if isinstance(slot, int):

            @pl.when(has_prev)
            def _():
                copy.wait_recv()

        else:
            copy.wait_recv()

    for n in range(PIECES):
        arrived(other, n)

        @pl.when(has_next)
        def _():
            send_other(n)

    for n in range(EARLY, PIECES):

        @pl.when(has_next & (core == 0))
        def _():
            send_own(n)

    for n in range(PIECES):

        @pl.when(far_next)
        def _():
            c, rows = piece(n)
            send_kv(kv.at[1, c, rows], 4, 4, n, far_ahead)

    for copy in acts:
        copy.wait_recv()
    turn_queries(other)
    turn_keys(other)

    forward([(other, other, 4 * other), (1, 0, 5)])

    for n in range(PIECES):
        arrived(3, n)

        @pl.when(passes_on)
        def _():
            c, rows = piece(n)
            send_kv(kv.at[3, c, rows], 4, 3, n, ahead)

    turn_keys(3)
    forward([(1, 3, 6), (0, 3, 1)])
    for n in range(PIECES):
        arrived(2, n)
    turn_keys(2)

    forward([(1, 2, 7), (0, 2, 2)])
    outs = []

    def hand_out(stage, dst, n, qs):
        here = pltpu.make_async_copy(
            stage.at[qs], dst.at[:, span_cols(core)], local_sem.at[n]
        )
        there = remote(
            stage.at[qs], dst.at[:, span_cols(core)], out_send.at[n], out_recv.at[n], partner
        )

        @pl.when(core == qs)
        def _():
            here.start()

        @pl.when(core != qs)
        def _():
            there.start()

        if qs == 0:
            outs.append((here, there))

    def send_gradient(slot, which, dst, extra=None, pieces=range(PIECES)):
        for n in pieces:
            c, rows = piece(n)
            value = grad_piece(slot, n)
            if extra is not None:

                @pl.when(passes_on)
                def _():
                    remote(
                        g_out.at[0, c, rows], extra.at[c, rows],
                        g_send.at[0, n], g_recv.at[0, n], partner,
                    ).wait_recv()

                value = value + extra[c, rows].astype(F32)
            g_out[which, c, rows] = value.astype(BF16)

            near = has_prev
            if which == 0:
                near = has_prev & (place_in_run > 0)

                @pl.when(far_prev)
                def _():
                    remote(
                        g_out.at[which, c, rows], g_direct.at[c, rows],
                        g_send.at[which, n], g_recv.at[4, n], far_behind,
                    ).start()

            @pl.when(near)
            def _():
                remote(
                    g_out.at[which, c, rows], dst.at[c, rows],
                    g_send.at[which, n], g_recv.at[which, n], behind,
                ).start()

    finish_forward(1)
    hand_out(o_stage, o_ref, 0, 1)
    for n in range(PIECES // 2):
        arrived(4, n)

    def last_values():
        for n in range(PIECES // 2, PIECES):
            arrived(4, n)
        turn_keys(4)

    forward([(0, 4, 3)], last_values)
    finish_forward(0)
    hand_out(o_stage, o_ref, 0, 0)
    halves = (range(PIECES // 2), range(PIECES // 2, PIECES))
    backward(
        [(0, 4, 3)],
        lambda: send_gradient(4, 0, g_relay, pieces=halves[1]),
        lambda: send_gradient(4, 0, g_relay, pieces=halves[0]),
    )
    backward([(1, 2, 7), (0, 2, 2)])
    send_gradient(2, 1, g_far.at[0])
    backward([(1, 3, 6), (0, 3, 1)])
    send_gradient(3, 2, g_far.at[1], g_relay)
    backward([(1, 0, 5), (1, 1, 4), (0, 0, 0)])
    finish_backward(1)
    hand_out(dq_stage, dq_ref, 1, 1)
    finish_backward(0)
    hand_out(dq_stage, dq_ref, 1, 0)

    grads = (gk_ref, gv_ref)
    ends = []
    for slot in range(2):
        for n in range(PIECES):
            c, rows = piece(n)

            @pl.when(has_next)
            def _():
                remote(
                    g_out.at[1 + slot, c, rows], g_far.at[slot, c, rows],
                    g_send.at[1 + slot, n], g_recv.at[1 + slot, n], partner,
                ).wait_recv()

            value = grad_piece(slot, n) + g_far[slot, c, rows].astype(F32)
            if slot == 1:

                @pl.when(far_next)
                def _():
                    remote(
                        g_out.at[0, c, rows], g_direct.at[c, rows],
                        g_send.at[0, n], g_recv.at[4, n], partner,
                    ).wait_recv()

                value = value + g_direct[c, rows].astype(F32)
            g_end[slot, c, rows] = value.astype(BF16)
            dst = grads[c].at[rows, head_cols(core)]
            here = pltpu.make_async_copy(g_end.at[slot, c, rows], dst, end_sem.at[n])
            there = remote(
                g_end.at[slot, c, rows], dst, g_send.at[3, n], g_recv.at[3, n], partner
            )

            @pl.when(core == slot)
            def _():
                here.start()

            @pl.when(core != slot)
            def _():
                there.start()

            if slot == 1:
                ends.append((here, there))
    for here, there in outs + ends:
        here.wait()
        there.wait()
    for copy in sent + acts:
        copy.wait_send()
    for n in range(PIECES):
        c, rows = piece(n)

        def gone(which):
            remote(
                kv.at[0, c, rows], kv.at[0, c, rows],
                kv_send.at[which, n], kv_recv.at[0, n], partner,
            ).wait_send()

        def gone_gradient(which):
            remote(
                g_out.at[which, c, rows], g_relay.at[c, rows],
                g_send.at[which, n], g_recv.at[0, n], partner,
            ).wait_send()

        @pl.when(has_next)
        def _():
            gone(0)
            gone(2)

        @pl.when(passes_on)
        def _():
            gone(3)

        @pl.when(far_next)
        def _():
            gone(4)

        @pl.when(has_prev)
        def _():
            for which in range(3):
                gone_gradient(which)


def copy_kernel(*refs):
    half = len(refs) // 2
    copies = [
        pltpu.make_async_copy(refs[n], refs[half + n], refs[-1].at[n]) for n in range(half)
    ]
    for copy in copies:
        copy.start()
    for copy in copies:
        copy.wait()


def per_device(queries, keys, values, output_gradient, lengths):
    count = lax.axis_size("ctx")
    width = KEY_VALUE_HEADS * HEAD
    wide = QUERY_HEADS * HEAD
    operands = (lengths, queries, keys, values, output_gradient)
    dma = pltpu.SemaphoreType.DMA
    vmem = pltpu.VMEM
    shapes = [
        jax.ShapeDtypeStruct((ROWS, wide), BF16),
        jax.ShapeDtypeStruct((ROWS, wide), BF16),
        jax.ShapeDtypeStruct((ROWS, width), BF16),
        jax.ShapeDtypeStruct((ROWS, width), BF16),
    ]
    results = pl.pallas_call(
        functools.partial(fused_kernel, count),
        out_shape=shapes,
        in_specs=[SMEM] + [HBM] * 4,
        out_specs=[ANY] * 4,
        scratch_shapes=[
            vmem((SLOTS, 2, ROWS, HEAD), BF16),
            vmem((SLOTS, HEAD, ROWS), BF16),
            vmem((SLOTS, HEAD + EXTRA, ROWS), BF16),
            vmem((2, LANES, HEAD), BF16),
            vmem((2, LANES, HEAD), BF16),
            vmem((2, HEAD, LANES), BF16),
            vmem((2, HEAD, LANES), BF16),
            vmem((8, ROWS, LANES), BF16),
            vmem((8, 8, LANES), F32),
            vmem((3, 8, LANES), F32),
            vmem((2, 8, LANES), F32),
            vmem((2, HEAD + EXTRA, LANES), F32),
            vmem((2, HEAD, LANES), F32),
            vmem((2, 8, LANES), F32),
            vmem((2, 8, LANES), F32),
            vmem((2, 8, ROWS), jnp.int32),
            vmem((SLOTS, 2, ROWS, HEAD), F32),
            vmem((2, ROWS, LANES), F32),
            vmem((2, ROWS, LANES), BF16),
            vmem((2, ROWS, LANES), BF16),
            vmem((2, ROWS, ROWS), F32),
            vmem((2, ROWS, SPAN), BF16),
            vmem((2, ROWS, SPAN), BF16),
            vmem((3, 2, ROWS, HEAD), BF16),
            vmem((2, ROWS, HEAD), BF16),
            vmem((2, ROWS, HEAD), BF16),
            vmem((2, 2, ROWS, HEAD), BF16),
            vmem((2, 2, ROWS, HEAD), BF16),
            dma((4,)),
            dma((PIECES,)),
            dma((5, PIECES)),
            dma((SLOTS, PIECES)),
            dma((2, GROUP)),
            dma((2, GROUP)),
            dma((2, GROUP)),
            dma((2,)),
            dma((2,)),
            dma((4, PIECES)),
            dma((5, PIECES)),
        ],
        compiler_params=pltpu.CompilerParams(
            collective_id=0, has_side_effects=True, vmem_limit_bytes=48 << 20
        ),
        name="attention",
    )(*(pltpu.with_memory_space_constraint(x, pltpu.HBM) for x in operands))
    return pl.pallas_call(
        copy_kernel,
        out_shape=[pltpu.HBM(x.shape, x.dtype) for x in shapes],
        in_specs=[ANY] * 4,
        out_specs=[HBM] * 4,
        scratch_shapes=[dma((4,))],
        name="place_results",
    )(*(pltpu.with_memory_space_constraint(x, pltpu.VMEM) for x in results))


def solution(mesh):
    split = P(("dp", "ctx"), None)
    return jax.shard_map(
        per_device,
        mesh=mesh,
        in_specs=(split, split, split, split, P("dp")),
        out_specs=(split, split, split, split),
        check_vma=False,
    )
```
